512 devices in a mesh: frames: 64 (over x, y, core), heads: 8 (over z).
Axes of the slice: x: 4, y: 8, z: 8, core: 2. Of those that a mesh axis runs over, the one named last changes fastest.
Arguments:
- query_states: bfloat16 [98304, 1024], P('frames', 'heads'), may hold values from -9 to 9
- key_states: bfloat16 [98304, 1024], P('frames', 'heads'), may hold values from -9 to 9
- value_states: bfloat16 [98304, 1024], P('frames', 'heads'), may hold values from -6 to 6
- pair_list: int32 [4096, 2], replicated, may hold values from 0 to 511, as said below
- out_weight: bfloat16 [1024, 1024], P('heads'), may hold values from -0.1875 to 0.1875
Outputs:
- attended: bfloat16 [98304, 1024], P('frames', 'heads')
The draws below stay inside these ranges and needn't reach their ends.
Inputs may be any that keep to these rules, and one draw needn't show every extreme that they name: `pair_list`: row r belongs to device r // 64 of frames: its first frame is held by that device (frames f * 8 to f * 8 + 7 on device f), its second frame j lies on device j // 8. Among the 64 rows of one device at most 1 have their second frame on any one device, and some device is reached exactly 1 times. The two frames of a row differ.
All inputs are finite; a program needn't handle non-finite values.
Results may differ from the reference program's by a relative error of at most 0.017.
Values may be sent and summed in bfloat16 or wider, within the bound.
A program may use at most 128 MiB of HBM per device.

```python
import math
import jax
import jax.numpy as jnp
from jax import lax

D = 1024
HEADS = 16
HDIM = 64
TOKF = 192
FR_DEV = 8
PAIR_DEV = 64
CAP = 1
FRAMES = 512
PAIRS = 4096
ROWS = 98304
N_HEADS = 8


def draw_query_states(key, part):
    key = jax.random.fold_in(key, 1)
    noises = jnp.clip(jax.random.normal(key, (FRAMES, TOKF, D), jnp.float32), -6.0, 6.0)
    result = 1.5 * noises
    return result.reshape(FRAMES * TOKF, D).astype(jnp.bfloat16)


def draw_key_states(key, part):
    key = jax.random.fold_in(key, 2)
    noises = jnp.clip(jax.random.normal(key, (FRAMES, TOKF, D), jnp.float32), -6.0, 6.0)
    result = 1.5 * noises
    return result.reshape(FRAMES * TOKF, D).astype(jnp.bfloat16)


def draw_pair_list(key, part):
    key = jax.random.fold_in(key, 7)
    device_count = FRAMES // FR_DEV
    pair_rows = PAIR_DEV
    subkeys = jax.random.split(key, 4)
    shuffled = jax.vmap(lambda subkey: jax.random.permutation(subkey, device_count * CAP))(jax.random.split(subkeys[0], device_count))
    targets = shuffled[:, :pair_rows] // CAP
    owners_col = jnp.arange(device_count)[:, None]
    first_loc = jax.random.randint(subkeys[1], (device_count, pair_rows), 0, FR_DEV)
    second_loc = jnp.minimum(jax.random.randint(subkeys[2], (device_count, pair_rows), 0, FR_DEV), jax.random.randint(subkeys[3], (device_count, pair_rows), 0, FR_DEV))
    clashes = (targets == owners_col) & (second_loc == first_loc)
    second_loc = jnp.where(clashes, (second_loc + 1) % FR_DEV, second_loc)
    first_frame = owners_col * FR_DEV + first_loc
    second_frame = targets * FR_DEV + second_loc
    return jnp.stack([first_frame, second_frame], axis=-1).reshape(device_count * pair_rows, 2).astype(jnp.int32)


def steps_of(rng, extent, cuts, low, high):
    def one(dim, parts):
        heights = jax.random.uniform(jax.random.fold_in(jax.random.fold_in(rng, 6), dim), (parts,), jnp.float32, low / len(cuts), high / len(cuts))
        return jnp.repeat(jnp.exp(heights), extent[dim] // parts).reshape((-1,) + (1,) * (len(extent) - dim - 1))

    level = one(*cuts[0])
    for cut in cuts[1:]:
        level = level * one(*cut)
    return level


def scatter_about(rng, extent, spread, reach, cuts=(), kind=jnp.bfloat16):
    gain = steps_of(rng, extent, cuts, -0.22, 0.18) if cuts else 1.0
    values = jax.random.normal(rng, extent, jnp.float32) * spread * gain
    return jnp.minimum(jnp.maximum(values, -reach), reach).astype(kind)


def setup_inputs(seed: int = 0) -> dict:
    keys = jax.random.split(jax.random.key(seed), 6)
    return {
        "query_states": draw_query_states(jax.random.fold_in(keys[5], 71), 0),
        "key_states": draw_key_states(jax.random.fold_in(keys[5], 71), 0),
        "value_states": scatter_about(keys[2], (ROWS, D), 1.0, 6.0, ((0, 64), (1, 8))),
        "pair_list": draw_pair_list(jax.random.fold_in(keys[5], 71), 0),
        "out_weight": scatter_about(keys[4], (D, D), D ** -0.5, 0.1875, ((0, 8),)),
    }


def attend(query_rows, key_rows, value_rows):
    number = query_rows.shape[0]
    queries = query_rows.astype(jnp.float32).reshape(number, TOKF, HEADS, HDIM)
    keyed = key_rows.astype(jnp.float32).reshape(number, TOKF, HEADS, HDIM)
    valued = value_rows.astype(jnp.float32).reshape(number, TOKF, HEADS, HDIM)
    scores = jnp.einsum('bqhd,bkhd->bhqk', queries, keyed) * (1.0 / math.sqrt(HDIM))
    highest = lax.optimization_barrier(jnp.max(scores, axis=-1, keepdims=True))
    exponent = jnp.exp(scores - highest)
    totals = lax.optimization_barrier(jnp.sum(exponent, axis=-1, keepdims=True))
    weights = (exponent / totals).astype(jnp.bfloat16)
    output = jnp.einsum('bhqk,bkhd->bqhd', weights.astype(jnp.float32), valued).astype(jnp.bfloat16)
    return (output.reshape(number, TOKF, D), (highest + jnp.log(totals))[..., 0])

def project(merged, out_weight):
    groups = N_HEADS
    group_width = D // groups

    def advance(summed, group_id):
        merged_cols = lax.dynamic_slice_in_dim(merged, group_id * group_width, group_width, 1)
        weight_rows = lax.dynamic_slice_in_dim(out_weight, group_id * group_width, group_width, 0)
        head_term = jnp.dot(merged_cols, weight_rows, preferred_element_type=jnp.float32).astype(jnp.bfloat16)
        head_term = lax.optimization_barrier(head_term)
        return (summed + head_term.astype(jnp.float32), None)
    summed, _ = lax.scan(advance, jnp.zeros((ROWS, D), jnp.float32), jnp.arange(groups, dtype=jnp.int32))
    return summed.astype(jnp.bfloat16)

def reference(query_states, key_states, value_states, pair_list, out_weight):
    frame_query = query_states.reshape(FRAMES, TOKF, D)
    frame_key = key_states.reshape(FRAMES, TOKF, D)
    frame_value = value_states.reshape(FRAMES, TOKF, D)
    own_block = math.gcd(FRAMES, 32)

    def own_part(block_id):
        start = block_id * own_block
        return attend(lax.dynamic_slice_in_dim(frame_query, start, own_block, 0), lax.dynamic_slice_in_dim(frame_key, start, own_block, 0), lax.dynamic_slice_in_dim(frame_value, start, own_block, 0))
    self_out, self_lse = lax.map(own_part, jnp.arange(FRAMES // own_block, dtype=jnp.int32))
    self_out = self_out.reshape(FRAMES, TOKF, D)
    self_lse = self_lse.reshape(FRAMES, HEADS, TOKF)
    pair_size = math.gcd(PAIRS, 128)
    pair_blocks = pair_list.reshape(PAIRS // pair_size, pair_size, 2)

    def advance(state, pair_block):
        highest, totals, summed = state
        first_frame = pair_block[:, 0]
        second_frame = pair_block[:, 1]
        ahead_out, ahead_lse = attend(frame_query[first_frame], frame_key[second_frame], frame_value[second_frame])
        behind_out, behind_lse = attend(frame_query[second_frame], frame_key[first_frame], frame_value[first_frame])
        frame_ids = jnp.concatenate([first_frame, second_frame], axis=0)
        outputs = jnp.concatenate([ahead_out, behind_out], axis=0)
        log_sums = jnp.concatenate([ahead_lse, behind_lse], axis=0)
        block_top = jax.ops.segment_max(log_sums, frame_ids, num_segments=FRAMES)
        new_top = jnp.maximum(highest, block_top)
        factor = jnp.exp(highest - new_top)
        weight = jnp.exp(log_sums - new_top[frame_ids])
        totals = totals * factor + jax.ops.segment_sum(weight, frame_ids, num_segments=FRAMES)
        weighted = outputs.astype(jnp.float32).reshape(-1, TOKF, HEADS, HDIM) * jnp.transpose(weight, (0, 2, 1))[..., None]
        summed = summed * jnp.transpose(factor, (0, 2, 1))[..., None] + jax.ops.segment_sum(weighted, frame_ids, num_segments=FRAMES)
        return ((new_top, totals, summed), None)
    start_state = (self_lse, jnp.ones_like(self_lse), self_out.astype(jnp.float32).reshape(FRAMES, TOKF, HEADS, HDIM))
    final_state, _ = lax.scan(advance, start_state, pair_blocks)
    highest, totals, summed = final_state
    merged = (summed / jnp.transpose(totals, (0, 2, 1))[..., None]).reshape(ROWS, D).astype(jnp.bfloat16)
    return project(merged, out_weight)
```

```python
import jax
import jax.numpy as jnp
from jax import lax
from jax.experimental import pallas as pl
from jax.experimental.pallas import tpu as pltpu
from jax.sharding import PartitionSpec as P

MESH = pl.DeviceIdType.MESH
BF = jnp.bfloat16
F32 = jnp.float32
TOKF, HDIM = 192, 64
X, Y, Z = 4, 8, 8
FR = 8
ROWS = FR * TOKF
RA = 80
WHOLE = (0, FR, 0, TOKF)
A_PART = (0, FR, 0, RA)
B_PART = (0, FR, RA, TOKF - RA)
A_HALF = {1: (0, FR // 2, 0, RA), -1: (FR // 2, FR // 2, 0, RA)}
B_HALF = {1: (0, FR // 2, RA, TOKF - RA), -1: (FR // 2, FR // 2, RA, TOKF - RA)}
UNITS = 136
PER = 8
LOOPS = UNITS // PER
DIRS = (1, -1)
ORDER = (0, -1, 1, -2, 2, -3, 3, 4)


def tables(pair_list, me):
    first = pair_list[:, 0].reshape(64, 64)
    second = pair_list[:, 1].reshape(64, 64)
    own_first = lax.dynamic_index_in_dim(first, me, 0, keepdims=False) - me * FR
    own_second = lax.dynamic_index_in_dim(second, me, 0, keepdims=False)
    mine = second // FR == me
    back_frame = jnp.sum(jnp.where(mine, second, 0), axis=1) - me * FR
    back_other = jnp.sum(jnp.where(mine, first, 0), axis=1)
    here = jnp.arange(FR, dtype=jnp.int32)
    frame = jnp.concatenate([here, own_first, back_frame])
    other = jnp.concatenate([here + me * FR, own_second, back_other])
    number = jnp.arange(UNITS, dtype=jnp.int32)
    ahead = (frame[None, :] < frame[:, None]) | (
        (frame[None, :] == frame[:, None]) & (number[None, :] < number[:, None])
    )
    place = jnp.sum(ahead.astype(jnp.int32), axis=1)
    hit = place[None, :] == number[:, None]
    frame_at = jnp.sum(jnp.where(hit, frame[None, :], 0), axis=1)
    other_at = jnp.sum(jnp.where(hit, other[None, :], 0), axis=1)
    same = jnp.sum(jnp.where(hit, (number >= FR).astype(jnp.int32)[None, :], 0), axis=1)
    last = jnp.sum((frame[None, :] <= number[:, None]).astype(jnp.int32), axis=1) - 1
    last = jnp.maximum(jnp.minimum(last, UNITS - 1), 0)
    source = other_at // FR
    fresh = jnp.where(same > 0, 0.0, -jnp.inf).astype(F32)
    return fresh[None, :], jnp.stack(
        [
            source % 2,
            source // (2 * Y),
            (source // 2) % Y,
            other_at % FR,
            frame_at,
            last,
        ]
    )


def kernel(
    tab, fresh, q_ref, k_ref, v_ref, w_ref, o_ref,
    buf0, buf1, slots, qz, mz0, mz1, wbuf, total, high, acc,
    send_sem, near_send, near_recv, recv_sem, w_send, w_recv, z_send, z_recv,
):
    bufs, mzs = (buf0, buf1), (mz0, mz1)
    me = lax.axis_index("frames")
    z = lax.axis_index("heads")
    x, y, c = me // (2 * Y), (me // 2) % Y, me % 2

    def ring(value, size):
        return lax.rem(value + 4 * size, size)

    def at(dx, dy):
        return (ring(x + dx, X) * (2 * Y) + ring(y + dy, Y) * 2 + c, z)

    partner = (x * (2 * Y) + y * 2 + (1 - c), z)

    def zat(dz):
        return (me, ring(z + dz, Z))

    barrier = pltpu.get_barrier_semaphore()
    peers = [at(1, 0), at(-1, 0), at(0, 1), at(0, -1), partner] + [zat(d) for d in range(1, Z)]
    for peer in peers:
        pl.semaphore_signal(barrier, inc=1, device_id=peer, device_id_type=MESH)

    lane = lax.broadcasted_iota(jnp.int32, (TOKF, 128), 1)
    low = lane < HDIM

    def prepare(head):
        for f in range(FR):
            rows = pl.ds(f * TOKF, TOKF)
            turned = pltpu.roll(v_ref[rows, :], HDIM, 1)
            keyed = k_ref[rows, :]
            block = jnp.where(low, keyed, turned) if head == 0 else jnp.where(low, turned, keyed)
            bufs[head][c, x, y, f] = block
            query = q_ref[rows, :] * jnp.asarray(0.125, BF)
            nil = jnp.zeros_like(query)
            qz[head, f] = jnp.where(low, query, nil) if head == 0 else jnp.where(low, nil, query)

    prepare(0)
    pl.semaphore_wait(barrier, len(peers))

    names = {}

    def sem_of(name):
        return names.setdefault(name, len(names))

    sent = {}
    near_sent = {}
    def view(head, spec):
        dx, dy, part = spec
        by = ring(y + dy, Y)
        frames, rows = pl.ds(part[0], part[1]), pl.ds(part[2], part[3])
        if dx is None:
            return bufs[head].at[c, :, by, frames, rows, :]
        return bufs[head].at[c, ring(x + dx, X), by, frames, rows, :]

    def link_copy(head, name, spec, device):
        number = sem_of(name)
        ref = view(head, spec)
        return pltpu.make_async_remote_copy(
            src_ref=ref, dst_ref=ref, send_sem=send_sem.at[number], recv_sem=recv_sem.at[head, number],
            device_id=device, device_id_type=MESH,
        )

    def near_copy(head, name, spec):
        number = near_names.setdefault(name, len(near_names))
        ref = view(head, spec)
        return pltpu.make_async_remote_copy(
            src_ref=ref, dst_ref=ref, send_sem=near_send.at[number], recv_sem=near_recv.at[head],
            device_id=partner, device_id_type=MESH,
        )

    def remote(head, name, spec, hop):
        if head == 1:
            link_copy(0, name, spec, partner).wait_send()
        link_copy(head, name, spec, at(*hop)).start()
        sent[name] = spec

    def arrive(head, name, spec):
        link_copy(head, name, spec, partner).wait_recv()

    def near(head, name, spec):
        if head == 1:
            near_copy(0, name, spec).wait_send()
        near_copy(head, name, spec).start()
        near_sent[name] = spec

    near_names = {}

    def start_x(head, k):
        for d in DIRS:
            remote(head, ("x1", k, d), (0, k, B_PART), (d, 0))

    def start_own(head):
        near(head, "own", (0, 0, WHOLE))
        for d in DIRS:
            remote(head, ("a1", d), (0, 0, A_PART), (d, 0))
        for d in DIRS:
            remote(head, ("b", 1, d), (0, 0, B_PART), (0, d))
        start_x(head, 0)

    def on_a1(head):
        for d in DIRS:
            arrive(head, ("a1", d), (-d, 0, A_PART))
            remote(head, ("a2", d), (-d, 0, A_HALF[d]), (d, 0))
            near(head, ("a1", d), (-d, 0, A_PART))

    def on_a2(head):
        for d in DIRS:
            arrive(head, ("a2", d), (2, 0, A_HALF[d]))
        for d in DIRS:
            remote(head, ("y", 1, d), (None, 0, A_PART), (0, d))
        near(head, "a2", (2, 0, A_PART))

    def on_b(head, k):
        if k < 4:
            for d in DIRS:
                arrive(head, ("b", k, d), (0, -d * k, B_PART))
                part = B_PART if k < 3 else B_HALF[d]
                remote(head, ("b", k + 1, d), (0, -d * k, part), (0, d))
                start_x(head, -d * k)
                near(head, ("b", k, d), (0, -d * k, B_PART))
        else:
            for d in DIRS:
                arrive(head, ("b", 4, d), (0, 4, B_HALF[d]))
            start_x(head, 4)
            near(head, ("b", 4), (0, 4, B_PART))

    def on_x1(head, k):
        for d in DIRS:
            arrive(head, ("x1", k, d), (-d, k, B_PART))
            remote(head, ("x2", k, d), (-d, k, B_HALF[d]), (d, 0))
            near(head, ("x1", k, d), (-d, k, B_PART))

    def on_x2(head, k):
        for d in DIRS:
            arrive(head, ("x2", k, d), (2, k, B_HALF[d]))
        near(head, ("x2", k), (2, k, B_PART))

    def on_y(head, k):
        if k < 4:
            for d in DIRS:
                arrive(head, ("y", k, d), (None, -d * k, A_PART))
                part = A_PART if k < 3 else A_HALF[d]
                remote(head, ("y", k + 1, d), (None, -d * k, part), (0, d))
                near(head, ("y", k, d), (None, -d * k, A_PART))
        else:
            for d in DIRS:
                arrive(head, ("y", 4, d), (None, 4, A_HALF[d]))
            near(head, ("y", 4), (None, 4, A_PART))

    def near_done(head):
        ref = bufs[head].at[1 - c]
        pltpu.make_async_remote_copy(
            src_ref=ref, dst_ref=ref, send_sem=near_send.at[0], recv_sem=near_recv.at[head],
            device_id=partner, device_id_type=MESH,
        ).wait_recv()

    def events(head):
        first = [lambda: on_a1(head), lambda: on_b(head, 1), lambda: on_a2(head)]
        first += [lambda k=k: on_b(head, k) for k in (2, 3, 4)]
        rest = []
        for i, k in enumerate(ORDER):
            rest.append(lambda k=k: on_x1(head, k))
            rest.append(lambda k=k: on_x2(head, k))
            if i % 2 == 1:
                rest.append(lambda k=i // 2 + 1: on_y(head, k))
        return first, rest

    def compute(head, iteration):
        buf = bufs[head]
        ones_at = low if head == 0 else jnp.logical_not(low)
        one, out = (0, HDIM) if head == 0 else (HDIM, 0)
        m, a = high[...], acc[...]
        for u in range(PER):
            t = iteration * PER + u
            kv = buf[tab[0, t], tab[1, t], tab[2, t], tab[3, t]]
            query = qz[head, tab[4, t]]
            s = lax.dot_general(kv, query, (((1,), (1,)), ((), ())), preferred_element_type=F32)
            m_prev = m + fresh[0, t]
            m = jnp.maximum(m_prev, jnp.max(s, axis=0, keepdims=True))
            p = jnp.exp(s - m).astype(BF)
            alpha = jnp.exp(m_prev - m)
            side = jnp.where(ones_at, jnp.ones_like(kv), kv)
            a = a * alpha + lax.dot_general(
                side, p, (((0,), (0,)), ((), ())), preferred_element_type=F32
            )
            slots[t] = (a[out : out + HDIM] / a[one : one + HDIM]).astype(BF)
        high[...] = m
        acc[...] = a

    def gather_merged(head):
        for f in range(FR // 2):
            both = jnp.concatenate([slots[tab[5, f]], slots[tab[5, f + FR // 2]]], axis=0)
            mzs[head][z, pl.ds(f * TOKF, TOKF), :] = both.T

    zrows = FR // 2 * TOKF
    z_half = {1: (0, zrows // 2), -1: (zrows // 2, zrows // 2)}

    def z_copy(head, k, d, source, part, device):
        ref = mzs[head].at[source, pl.ds(part[0], part[1]), :]
        number = 2 * (k - 1) + (d < 0)
        return pltpu.make_async_remote_copy(
            src_ref=ref, dst_ref=ref, send_sem=z_send.at[head, number], recv_sem=z_recv.at[head, number],
            device_id=device, device_id_type=MESH,
        )

    z_sent = []

    def z_start(head, k, d, source, part):
        copy = z_copy(head, k, d, source, part, zat(d))
        copy.start()
        z_sent.append(copy)

    def z_first(head):
        for d in DIRS:
            z_start(head, 1, d, z, (0, zrows))

    def on_z(head, k):
        sources = []
        for d in DIRS:
            source = ring(z - d * k, Z)
            z_copy(head, k, d, source, z_half[d] if k == 4 else (0, zrows), partner).wait_recv()
            if k < 4:
                z_start(head, k + 1, d, source, z_half[d] if k == 3 else (0, zrows))
                sources.append(source)
            elif d < 0:
                sources.append(source)
        for source in sources:
            project(head, source)

    def project(head, source, begin=False):
        w = wbuf[source, pl.ds(head * HDIM, HDIM), :]
        nil = jnp.zeros_like(w)
        wide = jnp.concatenate(
            [jnp.concatenate([w, nil], axis=1), jnp.concatenate([nil, w], axis=1)], axis=0
        )
        term = jnp.dot(mzs[head][source], wide, preferred_element_type=F32)
        total[...] = term if begin else total[...] + term

    w_copies = []
    for d in range(1, Z):
        target = ring(z + d, Z)
        start = pl.multiple_of(target * 128, 128)
        copy = pltpu.make_async_remote_copy(
            src_ref=w_ref.at[:, pl.ds(start, 128)], dst_ref=wbuf.at[z],
            send_sem=w_send.at[d - 1], recv_sem=w_recv.at[d - 1],
            device_id=zat(d), device_id_type=MESH,
        )

        w_copies.append(copy)

    start_own(0)
    for copy in w_copies:
        copy.start()
    prepare(1)
    wbuf[z] = w_ref[:, pl.ds(pl.multiple_of(z * 128, 128), 128)]
    high[...] = jnp.zeros_like(high)
    acc[...] = jnp.zeros_like(acc)

    first, rest = events(0)
    for event in first + rest[:-3]:
        event()
    start_own(1)
    for event in rest[-3:]:
        event()
    near_done(0)
    first, rest = events(1)
    for event in first:
        event()
    ahead = LOOPS

    @pl.loop(0, LOOPS)
    def _(iteration):
        for number, event in enumerate(rest[:ahead]):
            pl.when(iteration == number)(event)
        compute(0, iteration)

    rest = rest[ahead:]
    gather_merged(0)
    z_first(0)
    for copy in w_copies:
        copy.wait_recv()
    project(0, z, begin=True)
    steps = [lambda k=k: on_z(0, k) for k in (1, 2, 3, 4)]
    while rest or steps:
        if rest:
            rest.pop(0)()
        if steps:
            steps.pop(0)()
    near_done(1)

    @pl.loop(0, LOOPS)
    def _(iteration):
        compute(1, iteration)

    gather_merged(1)
    z_first(1)
    project(1, z)
    for k in (1, 2, 3, 4):
        on_z(1, k)
    for f in range(FR):
        half = f // (FR // 2)
        rows = (f % (FR // 2)) * TOKF
        o_ref[pl.ds(f * TOKF, TOKF), :] = total[
            pl.ds(rows, TOKF), pl.ds(half * 128, 128)
        ].astype(BF)
    for name, spec in sent.items():
        link_copy(1, name, spec, partner).wait_send()
    for name, spec in near_sent.items():
        near_copy(1, name, spec).wait_send()
    for copy in z_sent + w_copies:
        copy.wait_send()


def body(query_states, key_states, value_states, pair_list, out_weight):
    me = lax.axis_index("frames")
    fresh, tab = tables(pair_list, me)
    vmem = pl.BlockSpec(memory_space=pltpu.VMEM)
    smem = pl.BlockSpec(memory_space=pltpu.SMEM)
    return pl.pallas_call(
        kernel,
        out_shape=jax.ShapeDtypeStruct((ROWS, 128), BF),
        in_specs=[smem, smem, vmem, vmem, vmem, vmem],
        out_specs=vmem,
        scratch_shapes=[
            pltpu.VMEM((2, X, Y, FR, TOKF, 128), BF),
            pltpu.VMEM((2, X, Y, FR, TOKF, 128), BF),
            pltpu.VMEM((UNITS, HDIM, TOKF), BF),
            pltpu.VMEM((2, FR, TOKF, 128), BF),
            pltpu.VMEM((Z, FR // 2 * TOKF, 128), BF),
            pltpu.VMEM((Z, FR // 2 * TOKF, 128), BF),
            pltpu.VMEM((Z, 128, 128), BF),
            pltpu.VMEM((FR // 2 * TOKF, 256), F32),
            pltpu.VMEM((1, TOKF), F32),
            pltpu.VMEM((128, TOKF), F32),
            pltpu.SemaphoreType.DMA((52,)),
            pltpu.SemaphoreType.DMA((42,)),
            pltpu.SemaphoreType.DMA((2,)),
            pltpu.SemaphoreType.DMA((2, 52)),
            pltpu.SemaphoreType.DMA((7,)),
            pltpu.SemaphoreType.DMA((7,)),
            pltpu.SemaphoreType.DMA((2, 8)),
            pltpu.SemaphoreType.DMA((2, 8)),
        ],
        compiler_params=pltpu.CompilerParams(
            collective_id=0, has_side_effects=True, vmem_limit_bytes=63 * 2**20
        ),
        name="scene_attention",
    )(tab, fresh, query_states, key_states, value_states, out_weight)


def solution(mesh):
    placed = (
        P("frames", "heads"),
        P("frames", "heads"),
        P("frames", "heads"),
        P(),
        P("heads", None),
    )
    return jax.shard_map(
        body, mesh=mesh, in_specs=placed, out_specs=P("frames", "heads"), check_vma=False
    )
```

```python
import jax
import jax.numpy as jnp
from jax import lax
from jax.experimental import pallas as pl
from jax.experimental.pallas import tpu as pltpu
from jax.sharding import PartitionSpec as P

MESH = pl.DeviceIdType.MESH
BF = jnp.bfloat16
F32 = jnp.float32
TOKF, HDIM = 192, 64
X, Y, Z = 4, 8, 8
FR = 8
ROWS = FR * TOKF
RA = 80
WHOLE = (0, FR, 0, TOKF)
A_PART = (0, FR, 0, RA)
B_PART = (0, FR, RA, TOKF - RA)
A_HALF = {1: (0, FR // 2, 0, RA), -1: (FR // 2, FR // 2, 0, RA)}
B_HALF = {1: (0, FR // 2, RA, TOKF - RA), -1: (FR // 2, FR // 2, RA, TOKF - RA)}
UNITS = 136
PER = (8, 17)
DIRS = (1, -1)
AHEAD = (
    (0, ("a", 1)),
    (0, ("b", 1)),
    (0, ("w", 1)),
    (0, ("x", 0, 1)),
    (0, ("y", 0, 1)),
    (0, ("a", 2)),
    (0, ("w", 2)),
    (0, ("y", 1, 1)),
    (0, ("x", 1, 1)),
    (0, ("b", 2)),
    (0, ("w", 3)),
    (0, ("x", 0, 2)),
    (0, ("y", 0, 2)),
    (0, ("w", 4)),
    (0, ("y", 2, 1)),
    (0, ("x", 1, 2)),
    (0, ("y", 1, 2)),
    (0, ("x", 2, 1)),
    (0, ("b", 3)),
    (1, ("own", "y")),
    (0, ("y", 0, 3)),
    (0, ("x", 2, 2)),
    (0, ("y", 2, 2)),
    (0, ("y", 1, 3)),
    (0, ("x", 3, 1)),
    (1, ("own", "x")),
    (0, ("b", 4)),
    (1, ("b", 1)),
    (0, ("x", 3, 2)),
    (1, ("y", 0, 1)),
    (1, ("a", 1)),
    (0, ("y", 0, 4)),
    (0, ("y", 2, 3)),
    (1, ("x", 0, 1)),
    (0, ("y", 1, 4)),
    (0, ("x", 4, 1)),
    (1, ("b", 2)),
    (1, ("y", 0, 2)),
    (1, ("x", 1, 1)),
    (1, ("a", 2)),
    (1, ("y", 1, 1)),
    (1, ("x", 0, 2)),
    (0, ("y", 2, 4)),
    (0, ("x", 4, 2)),
)
BESIDE = (
    (2, (1, ("b", 3))),
    (6, (1, ("y", 0, 3))),
    (8, (1, ("x", 2, 1))),
    (8, (1, ("y", 2, 1))),
    (13, (1, ("x", 1, 2))),
    (15, (1, ("y", 1, 2))),
)
AFTER = (
    (1, ("b", 4)),
    (0, ("merge",)),
    (1, ("y", 0, 4)),
    (1, ("x", 3, 1)),
    (1, ("y", 2, 2)),
    (0, ("z", 1)),
    (1, ("x", 2, 2)),
    (1, ("y", 1, 3)),
    (1, ("x", 4, 1)),
    (1, ("y", 2, 3)),
    (0, ("z", 2)),
    (1, ("x", 3, 2)),
    (1, ("y", 1, 4)),
    (1, ("y", 2, 4)),
    (1, ("x", 4, 2)),
    (0, ("z", 3)),
    (0, ("z", 4)),
)


def tables(pair_list, me):
    first = pair_list[:, 0].reshape(64, 64)
    second = pair_list[:, 1].reshape(64, 64)
    own_first = lax.dynamic_index_in_dim(first, me, 0, keepdims=False) - me * FR
    own_second = lax.dynamic_index_in_dim(second, me, 0, keepdims=False)
    mine = second // FR == me
    back_frame = jnp.sum(jnp.where(mine, second, 0), axis=1) - me * FR
    back_other = jnp.sum(jnp.where(mine, first, 0), axis=1)
    here = jnp.arange(FR, dtype=jnp.int32)
    frame = jnp.concatenate([here, own_first, back_frame])
    other = jnp.concatenate([here + me * FR, own_second, back_other])
    number = jnp.arange(UNITS, dtype=jnp.int32)
    ahead = (frame[None, :] < frame[:, None]) | (
        (frame[None, :] == frame[:, None]) & (number[None, :] < number[:, None])
    )
    place = jnp.sum(ahead.astype(jnp.int32), axis=1)
    hit = place[None, :] == number[:, None]
    frame_at = jnp.sum(jnp.where(hit, frame[None, :], 0), axis=1)
    other_at = jnp.sum(jnp.where(hit, other[None, :], 0), axis=1)
    same = jnp.sum(jnp.where(hit, (number >= FR).astype(jnp.int32)[None, :], 0), axis=1)
    last = jnp.sum((frame[None, :] <= number[:, None]).astype(jnp.int32), axis=1) - 1
    last = jnp.maximum(jnp.minimum(last, UNITS - 1), 0)
    source = other_at // FR
    fresh = jnp.where(same > 0, 0.0, -jnp.inf).astype(F32)
    return fresh[None, :], jnp.stack(
        [
            source % 2,
            source // (2 * Y),
            (source // 2) % Y,
            other_at % FR,
            frame_at,
            last,
        ]
    )


def kernel(
    tab, fresh, q_ref, k_ref, v_ref, w_ref, o_ref,
    buf0, buf1, slots, qz, mz0, mz1, wbuf, total, high, acc,
    send_sem, near_send, near_recv, recv_sem, w_send, w_recv, z_send, z_recv,
):
    bufs, mzs = (buf0, buf1), (mz0, mz1)
    me = lax.axis_index("frames")
    z = lax.axis_index("heads")
    x, y, c = me // (2 * Y), (me // 2) % Y, me % 2

    def ring(value, size):
        return lax.rem(value + 4 * size, size)

    def at(dx, dy):
        return (ring(x + dx, X) * (2 * Y) + ring(y + dy, Y) * 2 + c, z)

    partner = (x * (2 * Y) + y * 2 + (1 - c), z)

    def zat(dz):
        return (me, ring(z + dz, Z))

    barrier = pltpu.get_barrier_semaphore()
    peers = [at(1, 0), at(-1, 0), at(0, 1), at(0, -1), partner] + [zat(1), zat(-1)]
    for peer in peers:
        pl.semaphore_signal(barrier, inc=1, device_id=peer, device_id_type=MESH)

    lane = lax.broadcasted_iota(jnp.int32, (TOKF, 128), 1)
    low = lane < HDIM

    def prepare(head):
        for f in range(FR):
            rows = pl.ds(f * TOKF, TOKF)
            turned = pltpu.roll(v_ref[rows, :], HDIM, 1)
            keyed = k_ref[rows, :]
            block = jnp.where(low, keyed, turned) if head == 0 else jnp.where(low, turned, keyed)
            bufs[head][c, x, y, f] = block
            query = q_ref[rows, :] * jnp.asarray(0.125, BF)
            nil = jnp.zeros_like(query)
            qz[head, f] = jnp.where(low, query, nil) if head == 0 else jnp.where(low, nil, query)

    prepare(0)
    pl.semaphore_wait(barrier, len(peers))

    names = {}

    def sem_of(name):
        return names.setdefault(name, len(names))

    sent = {}
    near_sent = {}
    def view(head, spec):
        dx, dy, part = spec
        by = ring(y + dy, Y)
        frames, rows = pl.ds(part[0], part[1]), pl.ds(part[2], part[3])
        if dx is None:
            return bufs[head].at[c, :, by, frames, rows, :]
        return bufs[head].at[c, ring(x + dx, X), by, frames, rows, :]

    def link_copy(head, name, spec, device):
        number = sem_of(name)
        ref = view(head, spec)
        return pltpu.make_async_remote_copy(
            src_ref=ref, dst_ref=ref, send_sem=send_sem.at[number], recv_sem=recv_sem.at[head, number],
            device_id=device, device_id_type=MESH,
        )

    def near_copy(head, name, spec):
        number = near_names.setdefault(name, len(near_names))
        ref = view(head, spec)
        return pltpu.make_async_remote_copy(
            src_ref=ref, dst_ref=ref, send_sem=near_send.at[number], recv_sem=near_recv.at[head],
            device_id=partner, device_id_type=MESH,
        )

    def remote(head, name, spec, hop):
        if head == 1:
            link_copy(0, name, spec, partner).wait_send()
        link_copy(head, name, spec, at(*hop)).start()
        sent[name] = spec

    def arrive(head, name, spec):
        link_copy(head, name, spec, partner).wait_recv()

    def near(head, name, spec):
        if head == 1:
            near_copy(0, name, spec).wait_send()
        near_copy(head, name, spec).start()
        near_sent[name] = spec

    near_names = {}

    def start_x(head, k):
        for d in DIRS:
            remote(head, ("x", k, 1, d), (0, k, B_PART), (d, 0))

    def start_y(head, j):
        for d in DIRS:
            remote(head, ("y", j, 1, d), (j, 0, A_PART), (0, d))

    def own_x(head):
        near(head, "own", (0, 0, WHOLE))
        for d in DIRS:
            remote(head, ("a", 1, d), (0, 0, A_PART), (d, 0))
        start_x(head, 0)

    def own_y(head):
        for d in DIRS:
            remote(head, ("b", 1, d), (0, 0, B_PART), (0, d))
        start_y(head, 0)

    def on_a(head, step):
        if step == 1:
            for d in DIRS:
                arrive(head, ("a", 1, d), (-d, 0, A_PART))
                remote(head, ("a", 2, d), (-d, 0, A_HALF[d]), (d, 0))
                start_y(head, -d)
                near(head, ("a", d), (-d, 0, A_PART))
        else:
            for d in DIRS:
                arrive(head, ("a", 2, d), (2, 0, A_HALF[d]))
            start_y(head, 2)
            near(head, "a", (2, 0, A_PART))

    def on_b(head, k):
        if k < 4:
            for d in DIRS:
                arrive(head, ("b", k, d), (0, -d * k, B_PART))
                part = B_PART if k < 3 else B_HALF[d]
                remote(head, ("b", k + 1, d), (0, -d * k, part), (0, d))
                start_x(head, -d * k)
                near(head, ("b", k, d), (0, -d * k, B_PART))
        else:
            for d in DIRS:
                arrive(head, ("b", 4, d), (0, 4, B_HALF[d]))
            start_x(head, 4)
            near(head, ("b", 4), (0, 4, B_PART))

    def on_x(head, distance, step):
        for k in sorted({-distance, distance}) if distance < 4 else [4]:
            for d in DIRS:
                if step == 1:
                    arrive(head, ("x", k, 1, d), (-d, k, B_PART))
                    remote(head, ("x", k, 2, d), (-d, k, B_HALF[d]), (d, 0))
                    near(head, ("x", k, d), (-d, k, B_PART))
                else:
                    arrive(head, ("x", k, 2, d), (2, k, B_HALF[d]))
            if step == 2:
                near(head, ("x", k), (2, k, B_PART))

    def on_y(head, distance, k):
        for j in (-1, 1) if distance == 1 else [distance]:
            for d in DIRS:
                if k < 4:
                    arrive(head, ("y", j, k, d), (j, -d * k, A_PART))
                    part = A_PART if k < 3 else A_HALF[d]
                    remote(head, ("y", j, k + 1, d), (j, -d * k, part), (0, d))
                    near(head, ("y", j, k, d), (j, -d * k, A_PART))
                else:
                    arrive(head, ("y", j, 4, d), (j, 4, A_HALF[d]))
            if k == 4:
                near(head, ("y", j, 4), (j, 4, A_PART))

    handlers = {"a": on_a, "b": on_b, "x": on_x, "y": on_y}

    def event(head, what):
        handlers[what[0]](head, *what[1:])

    def near_done(head):
        ref = bufs[head].at[1 - c]
        pltpu.make_async_remote_copy(
            src_ref=ref, dst_ref=ref, send_sem=near_send.at[0], recv_sem=near_recv.at[head],
            device_id=partner, device_id_type=MESH,
        ).wait_recv()

    def compute(head, iteration):
        buf, per = bufs[head], PER[head]
        ones_at = low if head == 0 else jnp.logical_not(low)
        one, out = (0, HDIM) if head == 0 else (HDIM, 0)
        units = [iteration * per + u for u in range(per)]

        def keys(t):
            return buf[tab[0, t], tab[1, t], tab[2, t], tab[3, t]]

        m, a = high[...], acc[...]
        scores, weights, scales = {}, {}, {}
        for step in range(per + 3):
            if step < per:
                t = units[step]
                scores[step] = lax.dot_general(
                    keys(t), qz[head, tab[4, t]], (((1,), (1,)), ((), ())), preferred_element_type=F32
                )
            u = step - 2
            if 0 <= u < per:
                s = scores.pop(u)
                m_prev = m + fresh[0, units[u]]
                m = jnp.maximum(m_prev, jnp.max(s, axis=0, keepdims=True))
                weights[u] = jnp.exp(s - m).astype(BF)
                scales[u] = jnp.exp(m_prev - m)
            u = step - 3
            if 0 <= u < per:
                kv = keys(units[u])
                side = jnp.where(ones_at, jnp.ones_like(kv), kv)
                a = a * scales.pop(u) + lax.dot_general(
                    side, weights.pop(u), (((0,), (0,)), ((), ())), preferred_element_type=F32
                )
                slots[units[u]] = (a[out : out + HDIM] * (1.0 / a[one : one + 1])).astype(BF)
        high[...] = m
        acc[...] = a

    chunk = FR // 4 * TOKF
    z_sent = []

    def ring_copy(ref, sems, k, d, device):
        return pltpu.make_async_remote_copy(
            src_ref=ref, dst_ref=ref, send_sem=sems[0].at[2 * (k - 1) + (d < 0)],
            recv_sem=sems[1].at[2 * (k - 1) + (d < 0)], device_id=device, device_id_type=MESH,
        )

    def z_copy(head, half, k, d, back):
        rows = pl.ds(half * chunk, chunk)
        if k == 4:
            rows = pl.ds(half * chunk + (d < 0) * (chunk // 2), chunk // 2)
        number = head * 2 + half
        ref = mzs[head].at[ring(z - d * (k - 1) - d * back, Z), rows, :]
        return ring_copy(ref, (z_send.at[number], z_recv.at[number]), k, d, zat(d))

    def w_copy(k, d, back):
        rows = pl.ds((d < 0) * HDIM, HDIM) if k == 4 else pl.ds(0, 2 * HDIM)
        ref = wbuf.at[ring(z - d * (k - 1) - d * back, Z), rows, :]
        return ring_copy(ref, (w_send, w_recv), k, d, zat(d))

    def w_start(k, d):
        w_copy(k, d, 0).start()
        z_sent.append(lambda: w_copy(k, d, 0))

    def on_w(k):
        for d in DIRS:
            w_copy(k, d, 1).wait_recv()
            if k < 4:
                w_start(k + 1, d)

    def z_start(head, half, k, d):
        z_copy(head, half, k, d, 0).start()
        z_sent.append(lambda: z_copy(head, half, k, d, 0))

    def merge(head):
        for half in (0, 1):
            for f in (2 * half, 2 * half + 1):
                both = jnp.concatenate([slots[tab[5, f]], slots[tab[5, f + FR // 2]]], axis=0)
                mzs[head][z, pl.ds(f * TOKF, TOKF), :] = both.T
            for d in DIRS:
                z_start(head, half, 1, d)
        for half in (0, 1):
            project(head, half, z, begin=head == 0)

    def on_z(head, k):
        for half in (0, 1):
            for d in DIRS:
                z_copy(head, half, k, d, 1).wait_recv()
                if k < 4:
                    z_start(head, half, k + 1, d)
            for d in DIRS if k < 4 else (1,):
                project(head, half, ring(z - d * k, Z))

    def project(head, half, source, begin=False):
        w = wbuf[source, pl.ds(head * HDIM, HDIM), pl.ds(pl.multiple_of(z * 128, 128), 128)]
        nil = jnp.zeros_like(w)
        wide = jnp.concatenate(
            [jnp.concatenate([w, nil], axis=1), jnp.concatenate([nil, w], axis=1)], axis=0
        )
        rows = pl.ds(half * chunk, chunk)
        term = jnp.dot(mzs[head][source, rows, :], wide, preferred_element_type=F32)
        total[rows, :] = term if begin else total[rows, :] + term

    def own(head, axis):
        (own_x if axis == "x" else own_y)(head)

    handlers.update(
        own=own, merge=merge, z=on_z, w=lambda head, k: on_w(k)
    )

    wbuf[z] = w_ref[...]
    own_x(0)
    own_y(0)
    for d in DIRS:
        w_start(1, d)
    prepare(1)
    high[...] = jnp.zeros_like(high)
    acc[...] = jnp.zeros_like(acc)
    for entry in AHEAD:
        event(*entry)
    near_done(0)

    @pl.loop(0, UNITS // PER[0])
    def _(iteration):
        for number, entry in BESIDE:
            pl.when(iteration == number)(lambda entry=entry: event(*entry))
        compute(0, iteration)

    for entry in AFTER:
        event(*entry)
    near_done(1)

    @pl.loop(0, UNITS // PER[1])
    def _(iteration):
        compute(1, iteration)

    merge(1)
    for k in (1, 2, 3, 4):
        on_z(1, k)
    for f in range(FR):
        side = f // (FR // 2)
        rows = (f % (FR // 2)) * TOKF
        o_ref[pl.ds(f * TOKF, TOKF), :] = total[
            pl.ds(rows, TOKF), pl.ds(side * 128, 128)
        ].astype(BF)
    for name, spec in sent.items():
        link_copy(1, name, spec, partner).wait_send()
    for name, spec in near_sent.items():
        near_copy(1, name, spec).wait_send()
    for copy in z_sent:
        copy().wait_send()


def body(query_states, key_states, value_states, pair_list, out_weight):
    me = lax.axis_index("frames")
    fresh, tab = tables(pair_list, me)
    vmem = pl.BlockSpec(memory_space=pltpu.VMEM)
    smem = pl.BlockSpec(memory_space=pltpu.SMEM)
    return pl.pallas_call(
        kernel,
        out_shape=jax.ShapeDtypeStruct((ROWS, 128), BF),
        in_specs=[smem, smem, vmem, vmem, vmem, vmem],
        out_specs=vmem,
        scratch_shapes=[
            pltpu.VMEM((2, X, Y, FR, TOKF, 128), BF),
            pltpu.VMEM((2, X, Y, FR, TOKF, 128), BF),
            pltpu.VMEM((UNITS, HDIM, TOKF), BF),
            pltpu.VMEM((2, FR, TOKF, 128), BF),
            pltpu.VMEM((Z, FR // 2 * TOKF, 128), BF),
            pltpu.VMEM((Z, FR // 2 * TOKF, 128), BF),
            pltpu.VMEM((Z, 128, 1024), BF),
            pltpu.VMEM((FR // 2 * TOKF, 256), F32),
            pltpu.VMEM((1, TOKF), F32),
            pltpu.VMEM((128, TOKF), F32),
            pltpu.SemaphoreType.DMA((76,)),
            pltpu.SemaphoreType.DMA((63,)),
            pltpu.SemaphoreType.DMA((2,)),
            pltpu.SemaphoreType.DMA((2, 76)),
            pltpu.SemaphoreType.DMA((8,)),
            pltpu.SemaphoreType.DMA((8,)),
            pltpu.SemaphoreType.DMA((4, 8)),
            pltpu.SemaphoreType.DMA((4, 8)),
        ],
        compiler_params=pltpu.CompilerParams(
            collective_id=0, has_side_effects=True, vmem_limit_bytes=63 * 2**20
        ),
        name="scene_attention",
    )(tab, fresh, query_states, key_states, value_states, out_weight)


def solution(mesh):
    placed = (
        P("frames", "heads"),
        P("frames", "heads"),
        P("frames", "heads"),
        P(),
        P("heads", None),
    )
    return jax.shard_map(
        body, mesh=mesh, in_specs=placed, out_specs=P("frames", "heads"), check_vma=False
    )
```

```python
import jax
import jax.numpy as jnp
from jax import lax
from jax.experimental import pallas as pl
from jax.experimental.pallas import tpu as pltpu
from jax.sharding import PartitionSpec as P

MESH = pl.DeviceIdType.MESH
BF = jnp.bfloat16
F32 = jnp.float32
TOKF, HDIM = 192, 64
X, Y, Z = 4, 8, 8
FR = 8
ROWS = FR * TOKF
DEVICES = 2 * X * Y
RA = 48
RB = TOKF - RA
HALVES = {1: (0, FR // 2), -1: (FR // 2, FR // 2)}
ALL = (0, FR)
OFFSETS = (0, -1, 1, -2, 2, -3, 3, 4)
UNITS = 136
PER = (8, 17)
COPIES = 148
DIRS = (1, -1)
AHEAD = (
    (0, ("a", 1)),
    (0, ("r", 0)),
    (0, ("w", 1)),
    (0, ("b", 1)),
    (0, ("a", 2)),
    (0, ("y", 0, 1)),
    (0, ("y", 1, 1)),
    (0, ("r", 1)),
    (0, ("w", 2)),
    (0, ("b", 2)),
    (0, ("y", 2, 1)),
    (0, ("w", 3)),
    (0, ("y", 0, 2)),
    (0, ("r", 2)),
    (0, ("w", 4)),
    (0, ("y", 1, 2)),
    (0, ("b", 3)),
    (0, ("y", 2, 2)),
    (0, ("y", 0, 3)),
    (0, ("r", 3)),
    (0, ("y", 1, 3)),
    (0, ("b", 4)),
    (0, ("y", 2, 3)),
    (0, ("y", 0, 4)),
    (0, ("y", 1, 4)),
    (0, ("r", 4)),
    (1, ("own", "x")),
    (1, ("own", "y")),
    (0, ("y", 2, 4)),
)
BESIDE = (
    (1, (1, ("a", 1))),
    (2, (1, ("r", 0))),
    (3, (1, ("b", 1))),
    (4, (1, ("y", 0, 1))),
    (6, (1, ("a", 2))),
    (8, (1, ("y", 1, 1))),
    (10, (1, ("r", 1))),
    (14, (1, ("b", 2))),
    (16, (1, ("y", 0, 2))),
)
AFTER = (
    (1, ("y", 2, 1)),
    (0, ("merge",)),
    (1, ("r", 2)),
    (1, ("y", 1, 2)),
    (0, ("z", 1)),
    (1, ("b", 3)),
    (1, ("y", 0, 3)),
    (1, ("y", 2, 2)),
    (0, ("z", 2)),
    (1, ("r", 3)),
    (1, ("y", 1, 3)),
    (1, ("b", 4)),
    (1, ("y", 0, 4)),
    (0, ("z", 3)),
    (1, ("y", 2, 3)),
    (1, ("y", 1, 4)),
    (1, ("r", 4)),
    (1, ("y", 2, 4)),
    (0, ("z", 4)),
)


def tables(pair_list, me):
    first = pair_list[:, 0].reshape(64, 64)
    second = pair_list[:, 1].reshape(64, 64)
    hit = (second // FR)[:, None, :] == jnp.arange(64, dtype=jnp.int32)[None, :, None]
    both = jnp.sum(jnp.where(hit, (first * 512 + second)[:, None, :], 0), axis=2)
    mine = lax.dynamic_index_in_dim(both, me, 0, keepdims=False)
    back = lax.dynamic_index_in_dim(both, me, 1, keepdims=False)
    here = jnp.arange(FR, dtype=jnp.int32)
    frame = jnp.concatenate([here, mine // 512 - me * FR, back % 512 - me * FR])
    other = jnp.concatenate([here + me * FR, mine % 512, back // 512])
    number = jnp.arange(UNITS, dtype=jnp.int32)
    ahead = (frame[None, :] < frame[:, None]) | (
        (frame[None, :] == frame[:, None]) & (number[None, :] < number[:, None])
    )
    place = jnp.sum(ahead.astype(jnp.int32), axis=1)
    kind = (number >= FR).astype(jnp.int32) + (number >= FR + 64).astype(jnp.int32)
    packed = (kind * 512 + other) * FR + frame
    packed = jnp.sum(jnp.where(place[None, :] == number[:, None], packed[None, :], 0), axis=1)
    frame_at, other_at, kind_at = packed % FR, (packed // FR) % 512, packed // (FR * 512)
    fresh = jnp.where(kind_at > 0, 0.0, -jnp.inf).astype(F32)
    last = jnp.sum((frame[None, :] <= number[:, None]).astype(jnp.int32), axis=1) - 1
    device = other_at // FR
    place_of = (device % 2) * (X * Y) + device // 2
    own_slot = 2 * DEVICES + frame_at
    slot = jnp.where(kind_at > 0, 2 * place_of + kind_at - 1, own_slot)
    asked = jnp.stack([both % FR, (both // 512) % FR])
    return asked, fresh[None, :], jnp.stack(
        [place_of, other_at % FR, slot // 2, slot % 2, frame_at, last, last, last]
    )


def kernel(
    asked, tab, fresh, q_ref, k_ref, v_ref, w_ref, o_ref,
    buf0, buf1, *rest,
):
    raws = (rest[:8], rest[8:16])
    (
        rec0, rec1, pack0, pack1, relay0, relay1, slots, qz, mz0, mz1, wbuf, total, high, acc, send_sem, near_recv, rec_recv, recv_sem, w_send, w_recv, z_send, z_recv,
    ) = rest[16:]
    bufs, mzs = (buf0, buf1), (mz0, mz1)
    recs, packs, relays = (rec0, rec1), (pack0, pack1), (relay0, relay1)
    me = lax.axis_index("frames")
    z = lax.axis_index("heads")
    x, y, c = me // (2 * Y), (me // 2) % Y, me % 2

    def ring(value, size):
        return lax.rem(value + 4 * size, size)

    def at(dx, dy, dc=0):
        return (ring(x + dx, X) * (2 * Y) + ring(y + dy, Y) * 2 + (c + dc) % 2, z)

    def slot_of(dx, dy):
        return c * (X * Y) + ring(x + dx, X) * Y + ring(y + dy, Y)

    partner = (x * (2 * Y) + y * 2 + (1 - c), z)

    def zat(dz):
        return (me, ring(z + dz, Z))

    barrier = pltpu.get_barrier_semaphore()
    peers = [at(1, 0), at(-1, 0), at(1, 0, 1), at(-1, 0, 1), at(0, 1), at(0, -1), partner] + [zat(1), zat(-1)]
    for peer in peers:
        pl.semaphore_signal(barrier, inc=1, device_id=peer, device_id_type=MESH)

    lane = lax.broadcasted_iota(jnp.int32, (TOKF, 128), 1)
    low = lane < HDIM

    def prepare(head):
        for f in range(FR):
            rows = pl.ds(f * TOKF, TOKF)
            turned = pltpu.roll(v_ref[rows, :], HDIM, 1)
            keyed = k_ref[rows, :]
            block = jnp.where(low, keyed, turned) if head == 0 else jnp.where(low, turned, keyed)
            bufs[head][slot_of(0, 0), f] = block[:RA]
            raws[head][0][f] = block[RA:]
            recs[head][DEVICES + f // 2, f % 2] = block[RA:]
            query = q_ref[rows, :] * jnp.asarray(0.125, BF)
            nil = jnp.zeros_like(query)
            qz[head, f] = jnp.where(low, query, nil) if head == 0 else jnp.where(low, nil, query)

    prepare(0)
    pl.semaphore_wait(barrier, len(peers))

    names = {}

    def sem_of(name):
        return names.setdefault(name, len(names))

    sent = {}
    def ends(head, name):
        kind = name[0]
        if kind in ("a", "y", "near"):
            dx, dy, part = {"a": a_spec, "y": y_spec, "near": near_spec}[kind](*name[1:])
            ref = bufs[head].at[slot_of(dx, dy), pl.ds(part[0], part[1])]
            return ref, ref
        if kind == "b":
            k, d = name[1:]
            there = -d * k if k < 4 else 4
            part = HALVES[d] if k == 4 else ALL
            frames = pl.ds(part[0], part[1])
            return (
                raws[head][OFFSETS.index(-d * (k - 1))].at[frames],
                raws[head][OFFSETS.index(there)].at[frames],
            )
        if kind == "p":
            number, to = name[1:]
            if to >= 5:
                return packs[head].at[number, to], relays[head].at[number, to - 5]
            return packs[head].at[number, to], recs[head].at[slot_of(0, OFFSETS[number])]
        number, d = name[1:]
        return (
            relays[head].at[number, 0 if d > 0 else 1],
            recs[head].at[slot_of(-d, OFFSETS[number])],
        )

    def a_spec(step, d):
        return (0, 0, ALL) if step == 1 else (-d, 0, HALVES[d])

    def y_spec(j, k, d):
        return (j, -d * (k - 1), ALL if k < 4 else HALVES[d])

    def near_spec(dx, dy):
        return (dx, dy, ALL)

    def hop(name):
        kind = name[0]
        if kind == "a":
            return (name[2], 0, 0)
        if kind in ("b", "y"):
            return (0, name[-1], 0)
        if kind == "near":
            return (0, 0, 1)
        if kind == "p":
            return ((0, 0, 1), (1, 0, 0), (1, 0, 1), (-1, 0, 0), (-1, 0, 1), (1, 0, 0), (-1, 0, 0))[name[2]]
        return (name[2], 0, 0 if name[2] > 0 else 1)

    def link_copy(head, name):
        number = sem_of(name)
        kind = name[0]
        if kind == "near":
            arrived = near_recv.at[head]
        elif kind == "r" or kind == "p" and name[2] < 5:
            arrived = rec_recv.at[head]
        else:
            arrived = recv_sem.at[head, number]
        source, target = ends(head, name)
        return pltpu.make_async_remote_copy(
            src_ref=source, dst_ref=target, send_sem=send_sem.at[number], recv_sem=arrived,
            device_id=at(*hop(name)), device_id_type=MESH,
        )

    def remote(head, *name):
        if head == 1:
            link_copy(0, name).wait_send()
        link_copy(head, name).start()
        sent[name] = True

    def arrive(head, ref, *name):
        pltpu.make_async_remote_copy(
            src_ref=ref, dst_ref=ref, send_sem=send_sem.at[sem_of(name)],
            recv_sem=recv_sem.at[head, sem_of(name)], device_id=partner, device_id_type=MESH,
        ).wait_recv()

    def a_block(head, dx, dy, part=ALL):
        return bufs[head].at[slot_of(dx, dy), pl.ds(part[0], part[1])]

    def device_at(dx, dy, dc):
        return at(dx, dy, dc)[0]

    def pack(head, number):
        source = device_at(0, OFFSETS[number], 0)
        targets = ((0, 0), (0, 1), (1, 0), (1, 1), (-1, 0), (-1, 1), (2, 0), (2, 1))
        for to, (dx, dc) in enumerate(targets):
            target = device_at(dx, 0, dc)
            wanted = (asked[0, target, source], asked[1, source, target])
            for j in (0, 1):
                rows = raws[head][number][wanted[j]]
                if to == 0:
                    recs[head][slot_of(0, OFFSETS[number]), j] = rows
                else:
                    packs[head][number, to - 1, j] = rows
        for to in (5, 6, 1, 2, 3, 4, 0):
            remote(head, "p", number, to)

    def on_r(head, distance):
        for number, offset in enumerate(OFFSETS):
            if abs(offset) == distance:
                for d in DIRS:
                    arrive(head, relays[head].at[number, 0 if d > 0 else 1], "p", number, 5 if d > 0 else 6)
                    remote(head, "r", number, d)

    def start_y(head, j):
        for d in DIRS:
            remote(head, "y", j, 1, d)

    def own_x(head):
        for d in DIRS:
            remote(head, "a", 1, d)
        pack(head, 0)
        remote(head, "near", 0, 0)

    def own_y(head):
        for d in DIRS:
            remote(head, "b", 1, d)
        start_y(head, 0)

    def on_a(head, step):
        if step == 1:
            for d in DIRS:
                arrive(head, a_block(head, -d, 0), "a", 1, d)
                remote(head, "a", 2, d)
                start_y(head, -d)
                remote(head, "near", -d, 0)
        else:
            for d in DIRS:
                arrive(head, a_block(head, 2, 0, HALVES[d]), "a", 2, d)
            start_y(head, 2)
            remote(head, "near", 2, 0)

    def on_b(head, k):
        for d in DIRS:
            number = OFFSETS.index(-d * k if k < 4 else 4)
            part = HALVES[d] if k == 4 else ALL
            arrive(head, raws[head][number].at[pl.ds(part[0], part[1])], "b", k, d)
            if k < 4:
                remote(head, "b", k + 1, d)
        for number, offset in enumerate(OFFSETS):
            if abs(offset) == k:
                pack(head, number)

    def on_y(head, distance, k):
        for j in (-1, 1) if distance == 1 else [distance]:
            for d in DIRS:
                if k < 4:
                    arrive(head, a_block(head, j, -d * k), "y", j, k, d)
                    remote(head, "y", j, k + 1, d)
                    remote(head, "near", j, -d * k)
                else:
                    arrive(head, a_block(head, j, 4, HALVES[d]), "y", j, 4, d)
            if k == 4:
                remote(head, "near", j, 4)

    handlers = {"a": on_a, "b": on_b, "r": on_r, "y": on_y}

    def event(head, what):
        handlers[what[0]](head, *what[1:])

    def near_done(head):
        for ref, arrived in (
            (bufs[head].at[pl.ds(0, DEVICES // 2)], near_recv),
            (recs[head].at[pl.ds(0, DEVICES - Y)], rec_recv),
        ):
            pltpu.make_async_remote_copy(
                src_ref=ref, dst_ref=ref, send_sem=send_sem.at[0], recv_sem=arrived.at[head],
                device_id=partner, device_id_type=MESH,
            ).wait_recv()

    def compute(head, iteration):
        per = PER[head]
        ones_at = low if head == 0 else jnp.logical_not(low)
        one, out = (0, HDIM) if head == 0 else (HDIM, 0)
        units = [iteration * per + u for u in range(per)]

        def keys(t):
            return jnp.concatenate(
                [bufs[head][tab[0, t], tab[1, t]], recs[head][tab[2, t], tab[3, t]]], axis=0
            )

        m, a = high[...], acc[...]
        scores, weights, scales = {}, {}, {}
        for step in range(per + 3):
            if step < per:
                t = units[step]
                scores[step] = lax.dot_general(
                    keys(t), qz[head, tab[4, t]], (((1,), (1,)), ((), ())), preferred_element_type=F32
                )
            u = step - 2
            if 0 <= u < per:
                s = scores.pop(u)
                m_prev = m + fresh[0, units[u]]
                m = jnp.maximum(m_prev, jnp.max(s, axis=0, keepdims=True))
                weights[u] = jnp.exp(s - m).astype(BF)
                scales[u] = jnp.exp(m_prev - m)
            u = step - 3
            if 0 <= u < per:
                kv = keys(units[u])
                side = jnp.where(ones_at, jnp.ones_like(kv), kv)
                a = a * scales.pop(u) + lax.dot_general(
                    side, weights.pop(u), (((0,), (0,)), ((), ())), preferred_element_type=F32
                )
                slots[units[u]] = (a[out : out + HDIM] * (1.0 / a[one : one + 1])).astype(BF)
        high[...] = m
        acc[...] = a

    chunk = FR // 4 * TOKF
    z_sent = []

    def ring_copy(ref, sems, k, d, device):
        return pltpu.make_async_remote_copy(
            src_ref=ref, dst_ref=ref, send_sem=sems[0].at[2 * (k - 1) + (d < 0)],
            recv_sem=sems[1].at[2 * (k - 1) + (d < 0)], device_id=device, device_id_type=MESH,
        )

    def z_copy(head, half, k, d, back):
        rows = pl.ds(half * chunk, chunk)
        if k == 4:
            rows = pl.ds(half * chunk + (d < 0) * (chunk // 2), chunk // 2)
        number = head * 2 + half
        ref = mzs[head].at[ring(z - d * (k - 1) - d * back, Z), rows, :]
        return ring_copy(ref, (z_send.at[number], z_recv.at[number]), k, d, zat(d))

    def w_copy(k, d, back):
        rows = pl.ds((d < 0) * HDIM, HDIM) if k == 4 else pl.ds(0, 2 * HDIM)
        ref = wbuf.at[ring(z - d * (k - 1) - d * back, Z), rows, :]
        return ring_copy(ref, (w_send, w_recv), k, d, zat(d))

    def w_start(k, d):
        w_copy(k, d, 0).start()
        z_sent.append(lambda: w_copy(k, d, 0))

    def on_w(k):
        for d in DIRS:
            w_copy(k, d, 1).wait_recv()
            if k < 4:
                w_start(k + 1, d)

    def z_start(head, half, k, d):
        z_copy(head, half, k, d, 0).start()
        z_sent.append(lambda: z_copy(head, half, k, d, 0))

    def merge(head):
        for half in (0, 1):
            for f in (2 * half, 2 * half + 1):
                both = jnp.concatenate([slots[tab[5, f]], slots[tab[5, f + FR // 2]]], axis=0)
                mzs[head][z, pl.ds(f * TOKF, TOKF), :] = both.T
            for d in DIRS:
                z_start(head, half, 1, d)
        for half in (0, 1):
            project(head, half, z, begin=head == 0)

    def on_z(head, k):
        for half in (0, 1):
            for d in DIRS:
                z_copy(head, half, k, d, 1).wait_recv()
                if k < 4:
                    z_start(head, half, k + 1, d)
            for d in DIRS if k < 4 else (1,):
                project(head, half, ring(z - d * k, Z))

    def project(head, half, source, begin=False):
        w = wbuf[source, pl.ds(head * HDIM, HDIM), pl.ds(pl.multiple_of(z * 128, 128), 128)]
        nil = jnp.zeros_like(w)
        wide = jnp.concatenate(
            [jnp.concatenate([w, nil], axis=1), jnp.concatenate([nil, w], axis=1)], axis=0
        )
        rows = pl.ds(half * chunk, chunk)
        term = jnp.dot(mzs[head][source, rows, :], wide, preferred_element_type=F32)
        total[rows, :] = term if begin else total[rows, :] + term

    def own(head, axis):
        (own_x if axis == "x" else own_y)(head)

    handlers.update(
        own=own, merge=merge, z=on_z, w=lambda head, k: on_w(k)
    )

    wbuf[z] = w_ref[...]
    own_x(0)
    own_y(0)
    for d in DIRS:
        w_start(1, d)
    prepare(1)
    high[...] = jnp.zeros_like(high)
    acc[...] = jnp.zeros_like(acc)
    for entry in AHEAD:
        event(*entry)
    near_done(0)

    @pl.loop(0, UNITS // PER[0])
    def _(iteration):
        for number, entry in BESIDE:
            pl.when(iteration == number)(lambda entry=entry: event(*entry))
        compute(0, iteration)

    for entry in AFTER:
        event(*entry)
    near_done(1)

    @pl.loop(0, UNITS // PER[1])
    def _(iteration):
        compute(1, iteration)

    merge(1)
    for k in (1, 2, 3, 4):
        on_z(1, k)
    for f in range(FR):
        side = f // (FR // 2)
        rows = (f % (FR // 2)) * TOKF
        o_ref[pl.ds(f * TOKF, TOKF), :] = total[
            pl.ds(rows, TOKF), pl.ds(side * 128, 128)
        ].astype(BF)
    for name in sent:
        link_copy(1, name).wait_send()
    for copy in z_sent:
        copy().wait_send()


def body(query_states, key_states, value_states, pair_list, out_weight):
    me = lax.axis_index("frames")
    asked, fresh, tab = tables(pair_list, me)
    vmem = pl.BlockSpec(memory_space=pltpu.VMEM)
    smem = pl.BlockSpec(memory_space=pltpu.SMEM)
    return pl.pallas_call(
        kernel,
        out_shape=jax.ShapeDtypeStruct((ROWS, 128), BF),
        in_specs=[smem, smem, smem, vmem, vmem, vmem, vmem],
        out_specs=vmem,
        scratch_shapes=[
            pltpu.VMEM((DEVICES, FR, RA, 128), BF),
            pltpu.VMEM((DEVICES, FR, RA, 128), BF),
            *[pltpu.VMEM((FR, RB, 128), BF) for _ in range(16)],
            pltpu.VMEM((DEVICES + FR // 2, 2, RB, 128), BF),
            pltpu.VMEM((DEVICES + FR // 2, 2, RB, 128), BF),
            pltpu.VMEM((8, 7, 2, RB, 128), BF),
            pltpu.VMEM((8, 7, 2, RB, 128), BF),
            pltpu.VMEM((8, 2, 2, RB, 128), BF),
            pltpu.VMEM((8, 2, 2, RB, 128), BF),
            pltpu.VMEM((UNITS, HDIM, TOKF), BF),
            pltpu.VMEM((2, FR, TOKF, 128), BF),
            pltpu.VMEM((Z, FR // 2 * TOKF, 128), BF),
            pltpu.VMEM((Z, FR // 2 * TOKF, 128), BF),
            pltpu.VMEM((Z, 128, 1024), BF),
            pltpu.VMEM((FR // 2 * TOKF, 256), F32),
            pltpu.VMEM((1, TOKF), F32),
            pltpu.VMEM((128, TOKF), F32),
            pltpu.SemaphoreType.DMA((COPIES,)),
            pltpu.SemaphoreType.DMA((2,)),
            pltpu.SemaphoreType.DMA((2,)),
            pltpu.SemaphoreType.DMA((2, COPIES)),
            pltpu.SemaphoreType.DMA((8,)),
            pltpu.SemaphoreType.DMA((8,)),
            pltpu.SemaphoreType.DMA((4, 8)),
            pltpu.SemaphoreType.DMA((4, 8)),
        ],
        compiler_params=pltpu.CompilerParams(
            collective_id=0, has_side_effects=True, vmem_limit_bytes=63 * 2**20
        ),
        name="scene_attention",
    )(asked, tab, fresh, query_states, key_states, value_states, out_weight)


def solution(mesh):
    placed = (
        P("frames", "heads"),
        P("frames", "heads"),
        P("frames", "heads"),
        P(),
        P("heads", None),
    )
    return jax.shard_map(
        body, mesh=mesh, in_specs=placed, out_specs=P("frames", "heads"), check_vma=False
    )
```

```python
import jax
import jax.numpy as jnp
from jax import lax
from jax.experimental import pallas as pl
from jax.experimental.pallas import tpu as pltpu
from jax.sharding import PartitionSpec as P

MESH = pl.DeviceIdType.MESH
BF = jnp.bfloat16
F32 = jnp.float32
TOKF, HDIM = 192, 64
X, Y, Z = 4, 8, 8
FR = 8
ROWS = FR * TOKF
DEVICES = 2 * X * Y
RA = 48
RB = TOKF - RA
HALVES = {1: (0, FR // 2), -1: (FR // 2, FR // 2)}
ALL = (0, FR)
OFFSETS = (0, -1, 1, -2, 2, -3, 3, 4)
UNITS = 136
FRESH = -1e30
PER = (8, 17)
COPIES = 148
DIRS = (1, -1)
AHEAD = (
    (0, ("a", 1)),
    (0, ("r", 0)),
    (0, ("w", 1)),
    (0, ("b", 1)),
    (0, ("a", 2)),
    (0, ("y", 0, 1)),
    (0, ("y", 1, 1)),
    (0, ("r", 1)),
    (0, ("w", 2)),
    (0, ("b", 2)),
    (0, ("y", 2, 1)),
    (0, ("w", 3)),
    (0, ("y", 0, 2)),
    (0, ("r", 2)),
    (0, ("y", 1, 2)),
    (0, ("w", 4)),
    (0, ("b", 3)),
    (0, ("y", 2, 2)),
    (0, ("y", 0, 3)),
    (0, ("r", 3)),
    (0, ("y", 1, 3)),
    (0, ("b", 4)),
    (0, ("y", 2, 3)),
    (0, ("y", 0, 4)),
    (1, ("own", "y")),
    (0, ("y", 1, 4)),
    (0, ("r", 4)),
    (1, ("own", "x")),
    (0, ("y", 2, 4)),
)
BESIDE = (
    (1, (1, ("b", 1))),
    (1, (1, ("a", 1))),
    (2, (1, ("r", 0))),
    (2, (1, ("y", 0, 1))),
    (9, (1, ("r", 1))),
    (10, (1, ("b", 2))),
    (14, (1, ("y", 1, 1))),
    (15, (1, ("a", 2))),
    (16, (1, ("y", 0, 2))),
)
AFTER = (
    (0, ("merge",)),
    (1, ("b", 3)),
    (1, ("r", 2)),
    (0, ("z", 1)),
    (1, ("y", 1, 2)),
    (1, ("y", 2, 1)),
    (1, ("y", 0, 3)),
    (1, ("r", 3)),
    (1, ("b", 4)),
    (0, ("z", 2)),
    (1, ("y", 1, 3)),
    (1, ("y", 2, 2)),
    (1, ("y", 0, 4)),
    (0, ("z", 3)),
    (1, ("y", 1, 4)),
    (1, ("y", 2, 3)),
    (1, ("r", 4)),
    (0, ("z", 4)),
    (1, ("y", 2, 4)),
)


def tables(pair_list, me):
    coded = jnp.sum(pair_list * jnp.array([512, 1], jnp.int32), axis=1).reshape(64, 64)
    hit = ((coded % 512) // FR)[:, None, :] == jnp.arange(64, dtype=jnp.int32)[None, :, None]
    both = jnp.sum(jnp.where(hit, coded[:, None, :], 0), axis=2)
    mine = lax.dynamic_index_in_dim(both, me, 0, keepdims=False)
    back = lax.dynamic_index_in_dim(both, me, 1, keepdims=False)
    here = jnp.arange(FR, dtype=jnp.int32)
    frame = jnp.concatenate([here, mine // 512 - me * FR, back % 512 - me * FR])
    other = jnp.concatenate([here + me * FR, mine % 512, back // 512])
    number = jnp.arange(UNITS, dtype=jnp.int32)
    ahead = (frame[None, :] < frame[:, None]) | (
        (frame[None, :] == frame[:, None]) & (number[None, :] < number[:, None])
    )
    place = jnp.sum(ahead.astype(jnp.int32), axis=1)
    device = other // FR
    place_of = (device % 2) * (X * Y) + device // 2
    behind = (number >= FR + 64).astype(jnp.int32)
    own = number < FR
    slot = jnp.where(own, 2 * DEVICES + frame, 2 * place_of + behind)
    unit = (((own.astype(jnp.int32) * 256 + slot) * 64 + place_of) * FR + other % FR) * FR + frame
    unit = jnp.sum(jnp.where(place[None, :] == number[:, None], unit[None, :], 0), axis=1)
    last = jnp.sum((frame[None, :] <= here[:, None]).astype(jnp.int32), axis=1) - 1
    return both, unit, last


def kernel(
    both, unit, last, q_ref, k_ref, v_ref, w_ref, o_ref,
    buf0, buf1, *rest,
):
    raws = (rest[:8], rest[8:16])
    (
        rec0, rec1, pack0, pack1, relay0, relay1, slots, qz, mz0, mz1, wbuf, total, high, acc, send_sem, near_recv, rec_recv, recv_sem, w_send, w_recv, z_send, z_recv,
    ) = rest[16:]
    bufs, mzs = (buf0, buf1), (mz0, mz1)
    recs, packs, relays = (rec0, rec1), (pack0, pack1), (relay0, relay1)
    me = lax.axis_index("frames")
    z = lax.axis_index("heads")
    x, y, c = me // (2 * Y), (me // 2) % Y, me % 2

    def ring(value, size):
        return lax.rem(value + 4 * size, size)

    def at(dx, dy, dc=0):
        return (ring(x + dx, X) * (2 * Y) + ring(y + dy, Y) * 2 + (c + dc) % 2, z)

    def slot_of(dx, dy):
        return c * (X * Y) + ring(x + dx, X) * Y + ring(y + dy, Y)

    partner = (x * (2 * Y) + y * 2 + (1 - c), z)

    def zat(dz):
        return (me, ring(z + dz, Z))

    barrier = pltpu.get_barrier_semaphore()
    peers = [at(1, 0), at(-1, 0), at(1, 0, 1), at(-1, 0, 1), at(0, 1), at(0, -1), partner] + [zat(1), zat(-1)]
    for peer in peers:
        pl.semaphore_signal(barrier, inc=1, device_id=peer, device_id_type=MESH)

    lane = lax.broadcasted_iota(jnp.int32, (TOKF, 128), 1)
    low = lane < HDIM

    def prepare(head):
        for f in range(FR):
            rows = pl.ds(f * TOKF, TOKF)
            turned = pltpu.roll(v_ref[rows, :], HDIM, 1)
            keyed = k_ref[rows, :]
            block = jnp.where(low, keyed, turned) if head == 0 else jnp.where(low, turned, keyed)
            bufs[head][slot_of(0, 0), f] = block[:RA]
            raws[head][0][f] = block[RA:]
            recs[head][DEVICES + f // 2, f % 2] = block[RA:]
            query = q_ref[rows, :] * jnp.asarray(0.125, BF)
            nil = jnp.zeros_like(query)
            qz[head, f] = jnp.where(low, query, nil) if head == 0 else jnp.where(low, nil, query)

    prepare(0)
    pl.semaphore_wait(barrier, len(peers))

    names = {}

    def sem_of(name):
        return names.setdefault(name, len(names))

    sent = {}
    def ends(head, name):
        kind = name[0]
        if kind in ("a", "y", "near"):
            dx, dy, part = {"a": a_spec, "y": y_spec, "near": near_spec}[kind](*name[1:])
            ref = bufs[head].at[slot_of(dx, dy), pl.ds(part[0], part[1])]
            return ref, ref
        if kind == "b":
            k, d = name[1:]
            there = -d * k if k < 4 else 4
            part = HALVES[d] if k == 4 else ALL
            frames = pl.ds(part[0], part[1])
            return (
                raws[head][OFFSETS.index(-d * (k - 1))].at[frames],
                raws[head][OFFSETS.index(there)].at[frames],
            )
        if kind == "p":
            number, to = name[1:]
            if to >= 5:
                return packs[head].at[number, to], relays[head].at[number, to - 5]
            return packs[head].at[number, to], recs[head].at[slot_of(0, OFFSETS[number])]
        number, d = name[1:]
        return (
            relays[head].at[number, 0 if d > 0 else 1],
            recs[head].at[slot_of(-d, OFFSETS[number])],
        )

    def a_spec(step, d):
        return (0, 0, ALL) if step == 1 else (-d, 0, HALVES[d])

    def y_spec(j, k, d):
        return (j, -d * (k - 1), ALL if k < 4 else HALVES[d])

    def near_spec(dx, dy):
        return (dx, dy, ALL)

    def hop(name):
        kind = name[0]
        if kind == "a":
            return (name[2], 0, 0)
        if kind in ("b", "y"):
            return (0, name[-1], 0)
        if kind == "near":
            return (0, 0, 1)
        if kind == "p":
            return ((0, 0, 1), (1, 0, 0), (1, 0, 1), (-1, 0, 0), (-1, 0, 1), (1, 0, 0), (-1, 0, 0))[name[2]]
        return (name[2], 0, 0 if name[2] > 0 else 1)

    def link_copy(head, name):
        number = sem_of(name)
        kind = name[0]
        if kind == "near":
            arrived = near_recv.at[head]
        elif kind == "r" or kind == "p" and name[2] < 5:
            arrived = rec_recv.at[head]
        else:
            arrived = recv_sem.at[head, number]
        source, target = ends(head, name)
        return pltpu.make_async_remote_copy(
            src_ref=source, dst_ref=target, send_sem=send_sem.at[number], recv_sem=arrived,
            device_id=at(*hop(name)), device_id_type=MESH,
        )

    def remote(head, *name):
        if head == 1:
            link_copy(0, name).wait_send()
        link_copy(head, name).start()
        sent[name] = True

    def arrive(head, ref, *name):
        pltpu.make_async_remote_copy(
            src_ref=ref, dst_ref=ref, send_sem=send_sem.at[sem_of(name)],
            recv_sem=recv_sem.at[head, sem_of(name)], device_id=partner, device_id_type=MESH,
        ).wait_recv()

    def a_block(head, dx, dy, part=ALL):
        return bufs[head].at[slot_of(dx, dy), pl.ds(part[0], part[1])]

    def device_at(dx, dy, dc):
        return at(dx, dy, dc)[0]

    def pack(head, number):
        source = device_at(0, OFFSETS[number], 0)
        targets = ((0, 0), (0, 1), (1, 0), (1, 1), (-1, 0), (-1, 1), (2, 0), (2, 1))
        for to, (dx, dc) in enumerate(targets):
            target = device_at(dx, 0, dc)
            wanted = (both[target, source] & 7, (both[source, target] >> 9) & 7)
            for j in (0, 1):
                rows = raws[head][number][wanted[j]]
                if to == 0:
                    recs[head][slot_of(0, OFFSETS[number]), j] = rows
                else:
                    packs[head][number, to - 1, j] = rows
        for to in (5, 6, 1, 2, 3, 4, 0):
            remote(head, "p", number, to)

    def on_r(head, distance):
        for number, offset in enumerate(OFFSETS):
            if abs(offset) == distance:
                for d in DIRS:
                    arrive(head, relays[head].at[number, 0 if d > 0 else 1], "p", number, 5 if d > 0 else 6)
                    remote(head, "r", number, d)

    def start_y(head, j):
        for d in DIRS:
            remote(head, "y", j, 1, d)

    def own_x(head):
        for d in DIRS:
            remote(head, "a", 1, d)
        pack(head, 0)
        remote(head, "near", 0, 0)

    def own_y(head):
        for d in DIRS:
            remote(head, "b", 1, d)
        start_y(head, 0)

    def on_a(head, step):
        if step == 1:
            for d in DIRS:
                arrive(head, a_block(head, -d, 0), "a", 1, d)
                remote(head, "a", 2, d)
                start_y(head, -d)
                remote(head, "near", -d, 0)
        else:
            for d in DIRS:
                arrive(head, a_block(head, 2, 0, HALVES[d]), "a", 2, d)
            start_y(head, 2)
            remote(head, "near", 2, 0)

    def on_b(head, k):
        for d in DIRS:
            number = OFFSETS.index(-d * k if k < 4 else 4)
            part = HALVES[d] if k == 4 else ALL
            arrive(head, raws[head][number].at[pl.ds(part[0], part[1])], "b", k, d)
            if k < 4:
                remote(head, "b", k + 1, d)
        for number, offset in enumerate(OFFSETS):
            if abs(offset) == k:
                pack(head, number)

    def on_y(head, distance, k):
        for j in (-1, 1) if distance == 1 else [distance]:
            for d in DIRS:
                if k < 4:
                    arrive(head, a_block(head, j, -d * k), "y", j, k, d)
                    remote(head, "y", j, k + 1, d)
                    remote(head, "near", j, -d * k)
                else:
                    arrive(head, a_block(head, j, 4, HALVES[d]), "y", j, 4, d)
            if k == 4:
                remote(head, "near", j, 4)

    handlers = {"a": on_a, "b": on_b, "r": on_r, "y": on_y}

    def event(head, what):
        handlers[what[0]](head, *what[1:])

    def near_done(head):
        for ref, arrived in (
            (bufs[head].at[pl.ds(0, DEVICES // 2)], near_recv),
            (recs[head].at[pl.ds(0, DEVICES - Y)], rec_recv),
        ):
            pltpu.make_async_remote_copy(
                src_ref=ref, dst_ref=ref, send_sem=send_sem.at[0], recv_sem=arrived.at[head],
                device_id=partner, device_id_type=MESH,
            ).wait_recv()

    def compute(head, iteration):
        per = PER[head]
        ones_at = low if head == 0 else jnp.logical_not(low)
        one, out = (0, HDIM) if head == 0 else (HDIM, 0)
        units = [iteration * per + u for u in range(per)]

        def keys(t):
            return jnp.concatenate(
                [bufs[head][(unit[t] >> 6) & 63, (unit[t] >> 3) & 7], recs[head][(unit[t] >> 13) & 127, (unit[t] >> 12) & 1]], axis=0
            )

        m, a = high[...], acc[...]
        scores, weights, scales = {}, {}, {}
        for step in range(per + 3):
            if step < per:
                t = units[step]
                scores[step] = lax.dot_general(
                    keys(t), qz[head, unit[t] & 7], (((1,), (1,)), ((), ())), preferred_element_type=F32
                )
            u = step - 2
            if 0 <= u < per:
                s = scores.pop(u)
                m_prev = m + (unit[units[u]] >> 20).astype(F32) * FRESH
                m = jnp.maximum(m_prev, jnp.max(s, axis=0, keepdims=True))
                weights[u] = jnp.exp(s - m).astype(BF)
                scales[u] = jnp.exp(m_prev - m)
            u = step - 3
            if 0 <= u < per:
                kv = keys(units[u])
                side = jnp.where(ones_at, jnp.ones_like(kv), kv)
                a = a * scales.pop(u) + lax.dot_general(
                    side, weights.pop(u), (((0,), (0,)), ((), ())), preferred_element_type=F32
                )
                slots[units[u]] = (a[out : out + HDIM] * (1.0 / a[one : one + 1])).astype(BF)
        high[...] = m
        acc[...] = a

    chunk = FR // 4 * TOKF
    z_sent = []

    def ring_copy(ref, sems, k, d, device):
        return pltpu.make_async_remote_copy(
            src_ref=ref, dst_ref=ref, send_sem=sems[0].at[2 * (k - 1) + (d < 0)],
            recv_sem=sems[1].at[2 * (k - 1) + (d < 0)], device_id=device, device_id_type=MESH,
        )

    def z_copy(head, half, k, d, back):
        rows = pl.ds(half * chunk, chunk)
        if k == 4:
            rows = pl.ds(half * chunk + (d < 0) * (chunk // 2), chunk // 2)
        number = head * 2 + half
        ref = mzs[head].at[ring(z - d * (k - 1) - d * back, Z), rows, :]
        return ring_copy(ref, (z_send.at[number], z_recv.at[number]), k, d, zat(d))

    def w_copy(k, d, back):
        rows = pl.ds((d < 0) * HDIM, HDIM) if k == 4 else pl.ds(0, 2 * HDIM)
        ref = wbuf.at[ring(z - d * (k - 1) - d * back, Z), rows, :]
        return ring_copy(ref, (w_send, w_recv), k, d, zat(d))

    def w_start(k, d):
        w_copy(k, d, 0).start()
        z_sent.append(lambda: w_copy(k, d, 0))

    def on_w(k):
        for d in DIRS:
            w_copy(k, d, 1).wait_recv()
            if k < 4:
                w_start(k + 1, d)

    def z_start(head, half, k, d):
        z_copy(head, half, k, d, 0).start()
        z_sent.append(lambda: z_copy(head, half, k, d, 0))

    def merge(head):
        for half in (0, 1):
            for f in (2 * half, 2 * half + 1):
                both = jnp.concatenate([slots[last[f]], slots[last[f + FR // 2]]], axis=0)
                mzs[head][z, pl.ds(f * TOKF, TOKF), :] = both.T
            for d in DIRS:
                z_start(head, half, 1, d)
        for half in (0, 1):
            project(head, half, z, begin=head == 0)

    def on_z(head, k):
        for half in (0, 1):
            for d in DIRS:
                z_copy(head, half, k, d, 1).wait_recv()
                if k < 4:
                    z_start(head, half, k + 1, d)
            for d in DIRS if k < 4 else (1,):
                project(head, half, ring(z - d * k, Z))

    def project(head, half, source, begin=False):
        w = wbuf[source, pl.ds(head * HDIM, HDIM), pl.ds(pl.multiple_of(z * 128, 128), 128)]
        nil = jnp.zeros_like(w)
        wide = jnp.concatenate(
            [jnp.concatenate([w, nil], axis=1), jnp.concatenate([nil, w], axis=1)], axis=0
        )
        rows = pl.ds(half * chunk, chunk)
        term = jnp.dot(mzs[head][source, rows, :], wide, preferred_element_type=F32)
        total[rows, :] = term if begin else total[rows, :] + term

    def own(head, axis):
        (own_x if axis == "x" else own_y)(head)

    handlers.update(
        own=own, merge=merge, z=on_z, w=lambda head, k: on_w(k)
    )

    wbuf[z] = w_ref[...]
    own_x(0)
    own_y(0)
    for d in DIRS:
        w_start(1, d)
    prepare(1)
    high[...] = jnp.zeros_like(high)
    acc[...] = jnp.zeros_like(acc)
    for entry in AHEAD:
        event(*entry)
    near_done(0)

    @pl.loop(0, UNITS // PER[0])
    def _(iteration):
        for number, entry in BESIDE:
            pl.when(iteration == number)(lambda entry=entry: event(*entry))
        compute(0, iteration)

    for entry in AFTER:
        event(*entry)
    near_done(1)

    @pl.loop(0, UNITS // PER[1])
    def _(iteration):
        compute(1, iteration)

    merge(1)
    for k in (1, 2, 3, 4):
        on_z(1, k)
    for f in range(FR):
        side = f // (FR // 2)
        rows = (f % (FR // 2)) * TOKF
        o_ref[pl.ds(f * TOKF, TOKF), :] = total[
            pl.ds(rows, TOKF), pl.ds(side * 128, 128)
        ].astype(BF)
    for name in sent:
        link_copy(1, name).wait_send()
    for copy in z_sent:
        copy().wait_send()


def body(query_states, key_states, value_states, pair_list, out_weight):
    me = lax.axis_index("frames")
    both, unit, last = tables(pair_list, me)
    vmem = pl.BlockSpec(memory_space=pltpu.VMEM)
    smem = pl.BlockSpec(memory_space=pltpu.SMEM)
    return pl.pallas_call(
        kernel,
        out_shape=jax.ShapeDtypeStruct((ROWS, 128), BF),
        in_specs=[smem, smem, smem, vmem, vmem, vmem, vmem],
        out_specs=vmem,
        scratch_shapes=[
            pltpu.VMEM((DEVICES, FR, RA, 128), BF),
            pltpu.VMEM((DEVICES, FR, RA, 128), BF),
            *[pltpu.VMEM((FR, RB, 128), BF) for _ in range(16)],
            pltpu.VMEM((DEVICES + FR // 2, 2, RB, 128), BF),
            pltpu.VMEM((DEVICES + FR // 2, 2, RB, 128), BF),
            pltpu.VMEM((8, 7, 2, RB, 128), BF),
            pltpu.VMEM((8, 7, 2, RB, 128), BF),
            pltpu.VMEM((8, 2, 2, RB, 128), BF),
            pltpu.VMEM((8, 2, 2, RB, 128), BF),
            pltpu.VMEM((UNITS, HDIM, TOKF), BF),
            pltpu.VMEM((2, FR, TOKF, 128), BF),
            pltpu.VMEM((Z, FR // 2 * TOKF, 128), BF),
            pltpu.VMEM((Z, FR // 2 * TOKF, 128), BF),
            pltpu.VMEM((Z, 128, 1024), BF),
            pltpu.VMEM((FR // 2 * TOKF, 256), F32),
            pltpu.VMEM((1, TOKF), F32),
            pltpu.VMEM((128, TOKF), F32),
            pltpu.SemaphoreType.DMA((COPIES,)),
            pltpu.SemaphoreType.DMA((2,)),
            pltpu.SemaphoreType.DMA((2,)),
            pltpu.SemaphoreType.DMA((2, COPIES)),
            pltpu.SemaphoreType.DMA((8,)),
            pltpu.SemaphoreType.DMA((8,)),
            pltpu.SemaphoreType.DMA((4, 8)),
            pltpu.SemaphoreType.DMA((4, 8)),
        ],
        compiler_params=pltpu.CompilerParams(
            collective_id=0, has_side_effects=True, vmem_limit_bytes=63 * 2**20
        ),
        name="scene_attention",
    )(both, unit, last, query_states, key_states, value_states, out_weight)


def solution(mesh):
    placed = (
        P("frames", "heads"),
        P("frames", "heads"),
        P("frames", "heads"),
        P(),
        P("heads", None),
    )
    return jax.shard_map(
        body, mesh=mesh, in_specs=placed, out_specs=P("frames", "heads"), check_vma=False
    )
```

```python
import jax
import jax.numpy as jnp
from jax import lax
from jax.experimental import pallas as pl
from jax.experimental.pallas import tpu as pltpu
from jax.sharding import PartitionSpec as P

MESH = pl.DeviceIdType.MESH
BF = jnp.bfloat16
F32 = jnp.float32
TOKF, HDIM = 192, 64
X, Y, Z = 4, 8, 8
FR = 8
ROWS = FR * TOKF
DEVICES = 2 * X * Y
RA = 48
RB = TOKF - RA
HALVES = {1: (0, FR // 2), -1: (FR // 2, FR // 2)}
ALL = (0, FR)
OFFSETS = (0, -1, 1, -2, 2, -3, 3, 4)
UNITS = 136
FRESH = -1e30
PER = (8, 34)
COPIES = 148
DIRS = (1, -1)
AHEAD = (
    (0, ("a", 1)),
    (0, ("r", 0)),
    (0, ("w", 1)),
    (0, ("b", 1)),
    (0, ("a", 2)),
    (0, ("y", 0, 1)),
    (0, ("y", 1, 1)),
    (0, ("r", 1)),
    (0, ("w", 2)),
    (0, ("b", 2)),
    (0, ("y", 2, 1)),
    (0, ("w", 3)),
    (0, ("y", 0, 2)),
    (0, ("r", 2)),
    (0, ("y", 1, 2)),
    (0, ("w", 4)),
    (0, ("b", 3)),
    (0, ("y", 2, 2)),
    (0, ("y", 0, 3)),
    (0, ("r", 3)),
    (0, ("y", 1, 3)),
    (0, ("b", 4)),
    (0, ("y", 2, 3)),
    (0, ("y", 0, 4)),
    (1, ("own", "y")),
    (0, ("y", 1, 4)),
    (0, ("r", 4)),
    (1, ("own", "x")),
    (0, ("y", 2, 4)),
)
BESIDE = (
    (1, (1, ("b", 1))),
    (1, (1, ("a", 1))),
    (2, (1, ("r", 0))),
    (2, (1, ("y", 0, 1))),
    (9, (1, ("r", 1))),
    (10, (1, ("b", 2))),
    (14, (1, ("y", 1, 1))),
    (15, (1, ("a", 2))),
    (16, (1, ("y", 0, 2))),
)
AFTER = (
    (0, ("merge",)),
    (1, ("b", 3)),
    (1, ("r", 2)),
    (0, ("z", 1)),
    (1, ("y", 1, 2)),
    (1, ("y", 2, 1)),
    (1, ("y", 0, 3)),
    (1, ("r", 3)),
    (1, ("b", 4)),
    (0, ("z", 2)),
    (1, ("y", 1, 3)),
    (1, ("y", 2, 2)),
    (1, ("y", 0, 4)),
    (0, ("z", 3)),
    (1, ("y", 1, 4)),
    (1, ("y", 2, 3)),
    (1, ("r", 4)),
    (0, ("z", 4)),
    (1, ("y", 2, 4)),
)


def tables(pair_list, me):
    coded = jnp.sum(pair_list * jnp.array([512, 1], jnp.int32), axis=1).reshape(64, 64)
    hit = ((coded % 512) // FR)[:, None, :] == jnp.arange(64, dtype=jnp.int32)[None, :, None]
    both = jnp.sum(jnp.where(hit, coded[:, None, :], 0), axis=2)
    mine = lax.dynamic_index_in_dim(both, me, 0, keepdims=False)
    back = lax.dynamic_index_in_dim(both, me, 1, keepdims=False)
    here = jnp.arange(FR, dtype=jnp.int32)
    frame = jnp.concatenate([here, mine // 512 - me * FR, back % 512 - me * FR])
    other = jnp.concatenate([here + me * FR, mine % 512, back // 512])
    number = jnp.arange(UNITS, dtype=jnp.int32)
    ahead = (frame[None, :] < frame[:, None]) | (
        (frame[None, :] == frame[:, None]) & (number[None, :] < number[:, None])
    )
    place = jnp.sum(ahead.astype(jnp.int32), axis=1)
    device = other // FR
    place_of = (device % 2) * (X * Y) + device // 2
    behind = (number >= FR + 64).astype(jnp.int32)
    own = number < FR
    slot = jnp.where(own, 2 * DEVICES + frame, 2 * place_of + behind)
    unit = (((own.astype(jnp.int32) * 256 + slot) * 64 + place_of) * FR + other % FR) * FR + frame
    unit = jnp.sum(jnp.where(place[None, :] == number[:, None], unit[None, :], 0), axis=1)
    last = jnp.sum((frame[None, :] <= here[:, None]).astype(jnp.int32), axis=1) - 1
    return both, unit, last


def kernel(
    both, unit, last, q_ref, k_ref, v_ref, w_ref, o_ref,
    buf0, buf1, *rest,
):
    raws = (rest[:8], rest[8:16])
    (
        rec0, rec1, pack0, pack1, relay0, relay1, slots, qz, mz0, mz1, wbuf, total, high, acc, send_sem, near_recv, rec_recv, recv_sem, w_send, w_recv, z_send, z_recv,
    ) = rest[16:]
    bufs, mzs = (buf0, buf1), (mz0, mz1)
    recs, packs, relays = (rec0, rec1), (pack0, pack1), (relay0, relay1)
    me = lax.axis_index("frames")
    z = lax.axis_index("heads")
    x, y, c = me // (2 * Y), (me // 2) % Y, me % 2

    def ring(value, size):
        return lax.rem(value + 4 * size, size)

    def at(dx, dy, dc=0):
        return (ring(x + dx, X) * (2 * Y) + ring(y + dy, Y) * 2 + (c + dc) % 2, z)

    def slot_of(dx, dy):
        return c * (X * Y) + ring(x + dx, X) * Y + ring(y + dy, Y)

    partner = (x * (2 * Y) + y * 2 + (1 - c), z)

    def zat(dz):
        return (me, ring(z + dz, Z))

    barrier = pltpu.get_barrier_semaphore()
    peers = [at(1, 0), at(-1, 0), at(1, 0, 1), at(-1, 0, 1), at(0, 1), at(0, -1), partner] + [zat(1), zat(-1)]
    for peer in peers:
        pl.semaphore_signal(barrier, inc=1, device_id=peer, device_id_type=MESH)

    lane = lax.broadcasted_iota(jnp.int32, (TOKF, 128), 1)
    low = lane < HDIM

    def prepare(head):
        for f in range(FR):
            rows = pl.ds(f * TOKF, TOKF)
            turned = pltpu.roll(v_ref[rows, :], HDIM, 1)
            keyed = k_ref[rows, :]
            block = jnp.where(low, keyed, turned) if head == 0 else jnp.where(low, turned, keyed)
            bufs[head][slot_of(0, 0), f] = block[:RA]
            raws[head][0][f] = block[RA:]
            recs[head][DEVICES + f // 2, f % 2] = block[RA:]
            query = q_ref[rows, :] * jnp.asarray(0.125, BF)
            nil = jnp.zeros_like(query)
            qz[head, f] = jnp.where(low, query, nil) if head == 0 else jnp.where(low, nil, query)

    prepare(0)
    pl.semaphore_wait(barrier, len(peers))

    names = {}

    def sem_of(name):
        return names.setdefault(name, len(names))

    sent = {}
    def ends(head, name):
        kind = name[0]
        if kind in ("a", "y", "near"):
            dx, dy, part = {"a": a_spec, "y": y_spec, "near": near_spec}[kind](*name[1:])
            ref = bufs[head].at[slot_of(dx, dy), pl.ds(part[0], part[1])]
            return ref, ref
        if kind == "b":
            k, d = name[1:]
            there = -d * k if k < 4 else 4
            part = HALVES[d] if k == 4 else ALL
            frames = pl.ds(part[0], part[1])
            return (
                raws[head][OFFSETS.index(-d * (k - 1))].at[frames],
                raws[head][OFFSETS.index(there)].at[frames],
            )
        if kind == "p":
            number, to = name[1:]
            if to >= 5:
                return packs[head].at[number, to], relays[head].at[number, to - 5]
            return packs[head].at[number, to], recs[head].at[slot_of(0, OFFSETS[number])]
        number, d = name[1:]
        return (
            relays[head].at[number, 0 if d > 0 else 1],
            recs[head].at[slot_of(-d, OFFSETS[number])],
        )

    def a_spec(step, d):
        return (0, 0, ALL) if step == 1 else (-d, 0, HALVES[d])

    def y_spec(j, k, d):
        return (j, -d * (k - 1), ALL if k < 4 else HALVES[d])

    def near_spec(dx, dy):
        return (dx, dy, ALL)

    def hop(name):
        kind = name[0]
        if kind == "a":
            return (name[2], 0, 0)
        if kind in ("b", "y"):
            return (0, name[-1], 0)
        if kind == "near":
            return (0, 0, 1)
        if kind == "p":
            return ((0, 0, 1), (1, 0, 0), (1, 0, 1), (-1, 0, 0), (-1, 0, 1), (1, 0, 0), (-1, 0, 0))[name[2]]
        return (name[2], 0, 0 if name[2] > 0 else 1)

    def link_copy(head, name):
        number = sem_of(name)
        kind = name[0]
        if kind == "near":
            arrived = near_recv.at[head]
        elif kind == "r" or kind == "p" and name[2] < 5:
            arrived = rec_recv.at[head]
        else:
            arrived = recv_sem.at[head, number]
        source, target = ends(head, name)
        return pltpu.make_async_remote_copy(
            src_ref=source, dst_ref=target, send_sem=send_sem.at[number], recv_sem=arrived,
            device_id=at(*hop(name)), device_id_type=MESH,
        )

    def remote(head, *name):
        if head == 1:
            link_copy(0, name).wait_send()
        link_copy(head, name).start()
        sent[name] = True

    def arrive(head, ref, *name):
        pltpu.make_async_remote_copy(
            src_ref=ref, dst_ref=ref, send_sem=send_sem.at[sem_of(name)],
            recv_sem=recv_sem.at[head, sem_of(name)], device_id=partner, device_id_type=MESH,
        ).wait_recv()

    def a_block(head, dx, dy, part=ALL):
        return bufs[head].at[slot_of(dx, dy), pl.ds(part[0], part[1])]

    def device_at(dx, dy, dc):
        return at(dx, dy, dc)[0]

    def pack(head, number):
        source = device_at(0, OFFSETS[number], 0)
        targets = ((0, 0), (0, 1), (1, 0), (1, 1), (-1, 0), (-1, 1), (2, 0), (2, 1))
        for to, (dx, dc) in enumerate(targets):
            target = device_at(dx, 0, dc)
            wanted = (both[target, source] & 7, (both[source, target] >> 9) & 7)
            for j in (0, 1):
                rows = raws[head][number][wanted[j]]
                if to == 0:
                    recs[head][slot_of(0, OFFSETS[number]), j] = rows
                else:
                    packs[head][number, to - 1, j] = rows
        for to in (5, 6, 1, 2, 3, 4, 0):
            remote(head, "p", number, to)

    def on_r(head, distance):
        for number, offset in enumerate(OFFSETS):
            if abs(offset) == distance:
                for d in DIRS:
                    arrive(head, relays[head].at[number, 0 if d > 0 else 1], "p", number, 5 if d > 0 else 6)
                    remote(head, "r", number, d)

    def start_y(head, j):
        for d in DIRS:
            remote(head, "y", j, 1, d)

    def own_x(head):
        for d in DIRS:
            remote(head, "a", 1, d)
        pack(head, 0)
        remote(head, "near", 0, 0)

    def own_y(head):
        for d in DIRS:
            remote(head, "b", 1, d)
        start_y(head, 0)

    def on_a(head, step):
        if step == 1:
            for d in DIRS:
                arrive(head, a_block(head, -d, 0), "a", 1, d)
                remote(head, "a", 2, d)
                start_y(head, -d)
                remote(head, "near", -d, 0)
        else:
            for d in DIRS:
                arrive(head, a_block(head, 2, 0, HALVES[d]), "a", 2, d)
            start_y(head, 2)
            remote(head, "near", 2, 0)

    def on_b(head, k):
        for d in DIRS:
            number = OFFSETS.index(-d * k if k < 4 else 4)
            part = HALVES[d] if k == 4 else ALL
            arrive(head, raws[head][number].at[pl.ds(part[0], part[1])], "b", k, d)
            if k < 4:
                remote(head, "b", k + 1, d)
        for number, offset in enumerate(OFFSETS):
            if abs(offset) == k:
                pack(head, number)

    def on_y(head, distance, k):
        for j in (-1, 1) if distance == 1 else [distance]:
            for d in DIRS:
                if k < 4:
                    arrive(head, a_block(head, j, -d * k), "y", j, k, d)
                    remote(head, "y", j, k + 1, d)
                    remote(head, "near", j, -d * k)
                else:
                    arrive(head, a_block(head, j, 4, HALVES[d]), "y", j, 4, d)
            if k == 4:
                remote(head, "near", j, 4)

    handlers = {"a": on_a, "b": on_b, "r": on_r, "y": on_y}

    def event(head, what):
        handlers[what[0]](head, *what[1:])

    def near_done(head):
        for ref, arrived in (
            (bufs[head].at[pl.ds(0, DEVICES // 2)], near_recv),
            (recs[head].at[pl.ds(0, DEVICES - Y)], rec_recv),
        ):
            pltpu.make_async_remote_copy(
                src_ref=ref, dst_ref=ref, send_sem=send_sem.at[0], recv_sem=arrived.at[head],
                device_id=partner, device_id_type=MESH,
            ).wait_recv()

    def compute(head, iteration):
        per = PER[head]
        ones_at = low if head == 0 else jnp.logical_not(low)
        one, out = (0, HDIM) if head == 0 else (HDIM, 0)
        units = [iteration * per + u for u in range(per)]

        def keys(t):
            return jnp.concatenate(
                [bufs[head][(unit[t] >> 6) & 63, (unit[t] >> 3) & 7], recs[head][(unit[t] >> 13) & 127, (unit[t] >> 12) & 1]], axis=0
            )

        m, a = high[...], acc[...]
        scores, weights, scales = {}, {}, {}
        for step in range(per + 5):
            if step < per:
                t = units[step]
                scores[step] = lax.dot_general(
                    keys(t), qz[head, unit[t] & 7], (((1,), (1,)), ((), ())), preferred_element_type=F32
                )
            u = step - 4
            if 0 <= u < per:
                s = scores.pop(u)
                m_prev = m + (unit[units[u]] >> 20).astype(F32) * FRESH
                m = jnp.maximum(m_prev, jnp.max(s, axis=0, keepdims=True))
                weights[u] = jnp.exp(s - m).astype(BF)
                scales[u] = jnp.exp(m_prev - m)
            u = step - 5
            if 0 <= u < per:
                kv = keys(units[u])
                side = jnp.where(ones_at, jnp.ones_like(kv), kv)
                a = a * scales.pop(u) + lax.dot_general(
                    side, weights.pop(u), (((0,), (0,)), ((), ())), preferred_element_type=F32
                )
                slots[units[u]] = (a[out : out + HDIM] * (1.0 / a[one : one + 1])).astype(BF)
        high[...] = m
        acc[...] = a

    chunk = FR // 4 * TOKF
    z_sent = []

    def ring_copy(ref, sems, k, d, device):
        return pltpu.make_async_remote_copy(
            src_ref=ref, dst_ref=ref, send_sem=sems[0].at[2 * (k - 1) + (d < 0)],
            recv_sem=sems[1].at[2 * (k - 1) + (d < 0)], device_id=device, device_id_type=MESH,
        )

    def z_copy(head, half, k, d, back):
        rows = pl.ds(half * chunk, chunk)
        if k == 4:
            rows = pl.ds(half * chunk + (d < 0) * (chunk // 2), chunk // 2)
        number = head * 2 + half
        ref = mzs[head].at[ring(z - d * (k - 1) - d * back, Z), rows, :]
        return ring_copy(ref, (z_send.at[number], z_recv.at[number]), k, d, zat(d))

    def w_copy(k, d, back):
        rows = pl.ds((d < 0) * HDIM, HDIM) if k == 4 else pl.ds(0, 2 * HDIM)
        ref = wbuf.at[ring(z - d * (k - 1) - d * back, Z), rows, :]
        return ring_copy(ref, (w_send, w_recv), k, d, zat(d))

    def w_start(k, d):
        w_copy(k, d, 0).start()
        z_sent.append(lambda: w_copy(k, d, 0))

    def on_w(k):
        for d in DIRS:
            w_copy(k, d, 1).wait_recv()
            if k < 4:
                w_start(k + 1, d)

    def z_start(head, half, k, d):
        z_copy(head, half, k, d, 0).start()
        z_sent.append(lambda: z_copy(head, half, k, d, 0))

    def merge(head):
        for half in (0, 1):
            for f in (2 * half, 2 * half + 1):
                both = jnp.concatenate([slots[last[f]], slots[last[f + FR // 2]]], axis=0)
                mzs[head][z, pl.ds(f * TOKF, TOKF), :] = both.T
            for d in DIRS:
                z_start(head, half, 1, d)
        for half in (0, 1):
            project(head, half, z, begin=head == 0)

    def on_z(head, k):
        for half in (0, 1):
            for d in DIRS:
                z_copy(head, half, k, d, 1).wait_recv()
                if k < 4:
                    z_start(head, half, k + 1, d)
        for half in (0, 1):
            for d in DIRS if k < 4 else (1,):
                project(head, half, ring(z - d * k, Z))

    def project(head, half, source, begin=False):
        w = wbuf[source, pl.ds(head * HDIM, HDIM), pl.ds(pl.multiple_of(z * 128, 128), 128)]
        nil = jnp.zeros_like(w)
        wide = jnp.concatenate(
            [jnp.concatenate([w, nil], axis=1), jnp.concatenate([nil, w], axis=1)], axis=0
        )
        rows = pl.ds(half * chunk, chunk)
        term = jnp.dot(mzs[head][source, rows, :], wide, preferred_element_type=F32)
        total[rows, :] = term if begin else total[rows, :] + term

    def own(head, axis):
        (own_x if axis == "x" else own_y)(head)

    handlers.update(
        own=own, merge=merge, z=on_z, w=lambda head, k: on_w(k)
    )

    wbuf[z] = w_ref[...]
    own_x(0)
    own_y(0)
    for d in DIRS:
        w_start(1, d)
    prepare(1)
    high[...] = jnp.zeros_like(high)
    acc[...] = jnp.zeros_like(acc)
    for entry in AHEAD:
        event(*entry)
    near_done(0)

    @pl.loop(0, UNITS // PER[0])
    def _(iteration):
        for number, entry in BESIDE:
            pl.when(iteration == number)(lambda entry=entry: event(*entry))
        compute(0, iteration)

    for entry in AFTER:
        event(*entry)
    near_done(1)

    @pl.loop(0, UNITS // PER[1])
    def _(iteration):
        compute(1, iteration)

    merge(1)
    for k in (1, 2, 3, 4):
        on_z(1, k)
    for f in range(FR):
        side = f // (FR // 2)
        rows = (f % (FR // 2)) * TOKF
        o_ref[pl.ds(f * TOKF, TOKF), :] = total[
            pl.ds(rows, TOKF), pl.ds(side * 128, 128)
        ].astype(BF)
    for name in sent:
        link_copy(1, name).wait_send()
    for copy in z_sent:
        copy().wait_send()


def body(query_states, key_states, value_states, pair_list, out_weight):
    me = lax.axis_index("frames")
    both, unit, last = tables(pair_list, me)
    vmem = pl.BlockSpec(memory_space=pltpu.VMEM)
    smem = pl.BlockSpec(memory_space=pltpu.SMEM)
    return pl.pallas_call(
        kernel,
        out_shape=jax.ShapeDtypeStruct((ROWS, 128), BF),
        in_specs=[smem, smem, smem, vmem, vmem, vmem, vmem],
        out_specs=vmem,
        scratch_shapes=[
            pltpu.VMEM((DEVICES, FR, RA, 128), BF),
            pltpu.VMEM((DEVICES, FR, RA, 128), BF),
            *[pltpu.VMEM((FR, RB, 128), BF) for _ in range(16)],
            pltpu.VMEM((DEVICES + FR // 2, 2, RB, 128), BF),
            pltpu.VMEM((DEVICES + FR // 2, 2, RB, 128), BF),
            pltpu.VMEM((8, 7, 2, RB, 128), BF),
            pltpu.VMEM((8, 7, 2, RB, 128), BF),
            pltpu.VMEM((8, 2, 2, RB, 128), BF),
            pltpu.VMEM((8, 2, 2, RB, 128), BF),
            pltpu.VMEM((UNITS, HDIM, TOKF), BF),
            pltpu.VMEM((2, FR, TOKF, 128), BF),
            pltpu.VMEM((Z, FR // 2 * TOKF, 128), BF),
            pltpu.VMEM((Z, FR // 2 * TOKF, 128), BF),
            pltpu.VMEM((Z, 128, 1024), BF),
            pltpu.VMEM((FR // 2 * TOKF, 256), F32),
            pltpu.VMEM((1, TOKF), F32),
            pltpu.VMEM((128, TOKF), F32),
            pltpu.SemaphoreType.DMA((COPIES,)),
            pltpu.SemaphoreType.DMA((2,)),
            pltpu.SemaphoreType.DMA((2,)),
            pltpu.SemaphoreType.DMA((2, COPIES)),
            pltpu.SemaphoreType.DMA((8,)),
            pltpu.SemaphoreType.DMA((8,)),
            pltpu.SemaphoreType.DMA((4, 8)),
            pltpu.SemaphoreType.DMA((4, 8)),
        ],
        compiler_params=pltpu.CompilerParams(
            collective_id=0, has_side_effects=True, vmem_limit_bytes=63 * 2**20
        ),
        name="scene_attention",
    )(both, unit, last, query_states, key_states, value_states, out_weight)


def solution(mesh):
    placed = (
        P("frames", "heads"),
        P("frames", "heads"),
        P("frames", "heads"),
        P(),
        P("heads", None),
    )
    return jax.shard_map(
        body, mesh=mesh, in_specs=placed, out_specs=P("frames", "heads"), check_vma=False
    )
```

```python
import jax
import jax.numpy as jnp
from jax import lax
from jax.experimental import pallas as pl
from jax.experimental.pallas import tpu as pltpu
from jax.sharding import PartitionSpec as P

MESH = pl.DeviceIdType.MESH
BF = jnp.bfloat16
F32 = jnp.float32
TOKF, HDIM = 192, 64
X, Y, Z = 4, 8, 8
FR = 8
ROWS = FR * TOKF
DEVICES = 2 * X * Y
RA = 48
RB = TOKF - RA
HALVES = {1: (0, FR // 2), -1: (FR // 2, FR // 2)}
ALL = (0, FR)
OFFSETS = (0, -1, 1, -2, 2, -3, 3, 4)
UNITS = 136
FRESH = -1e30
PER = (8, 34)
COPIES = 148
DIRS = (1, -1)
AHEAD = (
    (0, ("a", 1)),
    (0, ("r", 0)),
    (0, ("w", 1)),
    (0, ("b", 1)),
    (0, ("a", 2)),
    (0, ("y", 0, 1)),
    (0, ("y", 1, 1)),
    (0, ("r", 1)),
    (0, ("w", 2)),
    (0, ("b", 2)),
    (0, ("y", 2, 1)),
    (0, ("w", 3)),
    (0, ("y", 0, 2)),
    (0, ("r", 2)),
    (0, ("y", 1, 2)),
    (0, ("w", 4)),
    (0, ("b", 3)),
    (0, ("y", 2, 2)),
    (0, ("y", 0, 3)),
    (0, ("r", 3)),
    (0, ("y", 1, 3)),
    (0, ("b", 4)),
    (0, ("y", 2, 3)),
    (0, ("y", 0, 4)),
    (1, ("own", "y")),
    (0, ("y", 1, 4)),
    (0, ("r", 4)),
    (1, ("own", "x")),
    (0, ("y", 2, 4)),
)
BESIDE = (
    (1, (1, ("b", 1))),
    (1, (1, ("a", 1))),
    (2, (1, ("r", 0))),
    (2, (1, ("y", 0, 1))),
    (9, (1, ("r", 1))),
    (10, (1, ("b", 2))),
    (14, (1, ("y", 1, 1))),
    (15, (1, ("a", 2))),
    (16, (1, ("y", 0, 2))),
)
AFTER = (
    (0, ("merge",)),
    (1, ("b", 3)),
    (1, ("r", 2)),
    (0, ("z", 1)),
    (1, ("y", 1, 2)),
    (1, ("y", 2, 1)),
    (1, ("y", 0, 3)),
    (1, ("r", 3)),
    (1, ("b", 4)),
    (0, ("z", 2)),
    (1, ("y", 1, 3)),
    (1, ("y", 2, 2)),
    (1, ("y", 0, 4)),
    (0, ("z", 3)),
    (1, ("y", 1, 4)),
    (1, ("y", 2, 3)),
    (1, ("r", 4)),
    (0, ("z", 4)),
    (1, ("y", 2, 4)),
)


def tables(pair_list, me):
    coded = jnp.sum(pair_list * jnp.array([512, 1], jnp.int32), axis=1).reshape(64, 64)
    hit = ((coded % 512) // FR)[:, None, :] == jnp.arange(64, dtype=jnp.int32)[None, :, None]
    both = jnp.sum(jnp.where(hit, coded[:, None, :], 0), axis=2)
    mine = lax.dynamic_index_in_dim(both, me, 0, keepdims=False)
    back = lax.dynamic_index_in_dim(both, me, 1, keepdims=False)
    here = jnp.arange(FR, dtype=jnp.int32)
    frame = jnp.concatenate([here, mine // 512 - me * FR, back % 512 - me * FR])
    other = jnp.concatenate([here + me * FR, mine % 512, back // 512])
    number = jnp.arange(UNITS, dtype=jnp.int32)
    ahead = (frame[None, :] < frame[:, None]) | (
        (frame[None, :] == frame[:, None]) & (number[None, :] < number[:, None])
    )
    place = jnp.sum(ahead.astype(jnp.int32), axis=1)
    device = other // FR
    place_of = (device % 2) * (X * Y) + device // 2
    behind = (number >= FR + 64).astype(jnp.int32)
    own = number < FR
    slot = jnp.where(own, 2 * DEVICES + frame, 2 * place_of + behind)
    unit = (((own.astype(jnp.int32) * 256 + slot) * 64 + place_of) * FR + other % FR) * FR + frame
    unit = jnp.sum(jnp.where(place[None, :] == number[:, None], unit[None, :], 0), axis=1)
    last = jnp.sum((frame[None, :] <= here[:, None]).astype(jnp.int32), axis=1) - 1
    return both, unit, last


def kernel(
    both, unit, last, q_ref, k_ref, v_ref, w_ref, o_ref,
    buf0, buf1, *rest,
):
    raws = (rest[:8], rest[8:16])
    (
        rec0, rec1, pack0, pack1, relay0, relay1, slots, qz, mz0, mz1, wbuf, total, high, acc, send_sem, near_recv, rec_recv, recv_sem, w_send, w_recv, z_send, z_recv,
    ) = rest[16:]
    bufs, mzs = (buf0, buf1), (mz0, mz1)
    recs, packs, relays = (rec0, rec1), (pack0, pack1), (relay0, relay1)
    me = lax.axis_index("frames")
    z = lax.axis_index("heads")
    x, y, c = me // (2 * Y), (me // 2) % Y, me % 2

    def ring(value, size):
        return lax.rem(value + 4 * size, size)

    def at(dx, dy, dc=0):
        return (ring(x + dx, X) * (2 * Y) + ring(y + dy, Y) * 2 + (c + dc) % 2, z)

    def slot_of(dx, dy):
        return c * (X * Y) + ring(x + dx, X) * Y + ring(y + dy, Y)

    partner = (x * (2 * Y) + y * 2 + (1 - c), z)

    def zat(dz):
        return (me, ring(z + dz, Z))

    barrier = pltpu.get_barrier_semaphore()
    peers = [at(1, 0), at(-1, 0), at(1, 0, 1), at(-1, 0, 1), at(0, 1), at(0, -1), partner] + [zat(1), zat(-1)]
    for peer in peers:
        pl.semaphore_signal(barrier, inc=1, device_id=peer, device_id_type=MESH)

    lane = lax.broadcasted_iota(jnp.int32, (TOKF, 128), 1)
    low = lane < HDIM

    def prepare(head):
        for f in range(FR):
            rows = pl.ds(f * TOKF, TOKF)
            turned = pltpu.roll(v_ref[rows, :], HDIM, 1)
            keyed = k_ref[rows, :]
            block = jnp.where(low, keyed, turned) if head == 0 else jnp.where(low, turned, keyed)
            bufs[head][slot_of(0, 0), f] = block[:RA]
            raws[head][0][f] = block[RA:]
            recs[head][DEVICES + f // 2, f % 2] = block[RA:]
            query = q_ref[rows, :] * jnp.asarray(0.125, BF)
            nil = jnp.zeros_like(query)
            qz[head, f] = jnp.where(low, query, nil) if head == 0 else jnp.where(low, nil, query)

    prepare(0)
    pl.semaphore_wait(barrier, len(peers))

    names = {}

    def sem_of(name):
        return names.setdefault(name, len(names))

    sent = {}
    def ends(head, name):
        kind = name[0]
        if kind in ("a", "y", "near"):
            dx, dy, part = {"a": a_spec, "y": y_spec, "near": near_spec}[kind](*name[1:])
            ref = bufs[head].at[slot_of(dx, dy), pl.ds(part[0], part[1])]
            return ref, ref
        if kind == "b":
            k, d = name[1:]
            there = -d * k if k < 4 else 4
            part = HALVES[d] if k == 4 else ALL
            frames = pl.ds(part[0], part[1])
            return (
                raws[head][OFFSETS.index(-d * (k - 1))].at[frames],
                raws[head][OFFSETS.index(there)].at[frames],
            )
        if kind == "p":
            number, to = name[1:]
            if to >= 5:
                return packs[head].at[number, to], relays[head].at[number, to - 5]
            return packs[head].at[number, to], recs[head].at[slot_of(0, OFFSETS[number])]
        number, d = name[1:]
        return (
            relays[head].at[number, 0 if d > 0 else 1],
            recs[head].at[slot_of(-d, OFFSETS[number])],
        )

    def a_spec(step, d):
        return (0, 0, ALL) if step == 1 else (-d, 0, HALVES[d])

    def y_spec(j, k, d):
        return (j, -d * (k - 1), ALL if k < 4 else HALVES[d])

    def near_spec(dx, dy):
        return (dx, dy, ALL)

    def hop(name):
        kind = name[0]
        if kind == "a":
            return (name[2], 0, 0)
        if kind in ("b", "y"):
            return (0, name[-1], 0)
        if kind == "near":
            return (0, 0, 1)
        if kind == "p":
            return ((0, 0, 1), (1, 0, 0), (1, 0, 1), (-1, 0, 0), (-1, 0, 1), (1, 0, 0), (-1, 0, 0))[name[2]]
        return (name[2], 0, 0 if name[2] > 0 else 1)

    def link_copy(head, name):
        number = sem_of(name)
        kind = name[0]
        if kind == "near":
            arrived = near_recv.at[head]
        elif kind == "r" or kind == "p" and name[2] < 5:
            arrived = rec_recv.at[head]
        else:
            arrived = recv_sem.at[head, number]
        source, target = ends(head, name)
        return pltpu.make_async_remote_copy(
            src_ref=source, dst_ref=target, send_sem=send_sem.at[number], recv_sem=arrived,
            device_id=at(*hop(name)), device_id_type=MESH,
        )

    def remote(head, *name):
        if head == 1:
            link_copy(0, name).wait_send()
        link_copy(head, name).start()
        sent[name] = True

    def arrive(head, ref, *name):
        pltpu.make_async_remote_copy(
            src_ref=ref, dst_ref=ref, send_sem=send_sem.at[sem_of(name)],
            recv_sem=recv_sem.at[head, sem_of(name)], device_id=partner, device_id_type=MESH,
        ).wait_recv()

    def a_block(head, dx, dy, part=ALL):
        return bufs[head].at[slot_of(dx, dy), pl.ds(part[0], part[1])]

    def device_at(dx, dy, dc):
        return at(dx, dy, dc)[0]

    def pack(head, number):
        source = device_at(0, OFFSETS[number], 0)
        targets = ((0, 0), (0, 1), (1, 0), (1, 1), (-1, 0), (-1, 1), (2, 0), (2, 1))
        for to, (dx, dc) in enumerate(targets):
            target = device_at(dx, 0, dc)
            wanted = (both[target, source] & 7, (both[source, target] >> 9) & 7)
            for j in (0, 1):
                rows = raws[head][number][wanted[j]]
                if to == 0:
                    recs[head][slot_of(0, OFFSETS[number]), j] = rows
                else:
                    packs[head][number, to - 1, j] = rows
        for to in (5, 6, 1, 2, 3, 4, 0):
            remote(head, "p", number, to)

    def on_r(head, distance):
        for number, offset in enumerate(OFFSETS):
            if abs(offset) == distance:
                for d in DIRS:
                    arrive(head, relays[head].at[number, 0 if d > 0 else 1], "p", number, 5 if d > 0 else 6)
                    remote(head, "r", number, d)

    def start_y(head, j):
        for d in DIRS:
            remote(head, "y", j, 1, d)

    def own_x(head):
        for d in DIRS:
            remote(head, "a", 1, d)
        pack(head, 0)
        remote(head, "near", 0, 0)

    def own_y(head):
        for d in DIRS:
            remote(head, "b", 1, d)
        start_y(head, 0)

    def on_a(head, step):
        if step == 1:
            for d in DIRS:
                arrive(head, a_block(head, -d, 0), "a", 1, d)
                remote(head, "a", 2, d)
                start_y(head, -d)
                remote(head, "near", -d, 0)
        else:
            for d in DIRS:
                arrive(head, a_block(head, 2, 0, HALVES[d]), "a", 2, d)
            start_y(head, 2)
            remote(head, "near", 2, 0)

    def on_b(head, k):
        for d in DIRS:
            number = OFFSETS.index(-d * k if k < 4 else 4)
            part = HALVES[d] if k == 4 else ALL
            arrive(head, raws[head][number].at[pl.ds(part[0], part[1])], "b", k, d)
            if k < 4:
                remote(head, "b", k + 1, d)
        for number, offset in enumerate(OFFSETS):
            if abs(offset) == k:
                pack(head, number)

    def on_y(head, distance, k):
        for j in (-1, 1) if distance == 1 else [distance]:
            for d in DIRS:
                if k < 4:
                    arrive(head, a_block(head, j, -d * k), "y", j, k, d)
                    remote(head, "y", j, k + 1, d)
                    remote(head, "near", j, -d * k)
                else:
                    arrive(head, a_block(head, j, 4, HALVES[d]), "y", j, 4, d)
            if k == 4:
                remote(head, "near", j, 4)

    handlers = {"a": on_a, "b": on_b, "r": on_r, "y": on_y}

    def event(head, what):
        handlers[what[0]](head, *what[1:])

    def near_done(head):
        for ref, arrived in (
            (bufs[head].at[pl.ds(0, DEVICES // 2)], near_recv),
            (recs[head].at[pl.ds(0, DEVICES - Y)], rec_recv),
        ):
            pltpu.make_async_remote_copy(
                src_ref=ref, dst_ref=ref, send_sem=send_sem.at[0], recv_sem=arrived.at[head],
                device_id=partner, device_id_type=MESH,
            ).wait_recv()

    def compute(head, iteration):
        per = PER[head]
        ones_at = low if head == 0 else jnp.logical_not(low)
        one, out = (0, HDIM) if head == 0 else (HDIM, 0)
        units = [iteration * per + u for u in range(per)]

        def keys(t):
            return jnp.concatenate(
                [bufs[head][(unit[t] >> 6) & 63, (unit[t] >> 3) & 7], recs[head][(unit[t] >> 13) & 127, (unit[t] >> 12) & 1]], axis=0
            )

        m, a = high[...], acc[...]
        scores, weights, scales = {}, {}, {}
        for step in range(per + 5):
            if step < per:
                t = units[step]
                scores[step] = lax.dot_general(
                    keys(t), qz[head, unit[t] & 7], (((1,), (1,)), ((), ())), preferred_element_type=F32
                )
            u = step - 4
            if 0 <= u < per:
                s = scores.pop(u)
                m_prev = m + (unit[units[u]] >> 20).astype(F32) * FRESH
                m = jnp.maximum(m_prev, jnp.max(s, axis=0, keepdims=True))
                weights[u] = jnp.exp(s - m).astype(BF)
                scales[u] = jnp.exp(m_prev - m)
            u = step - 5
            if 0 <= u < per:
                kv = keys(units[u])
                side = jnp.where(ones_at, jnp.ones_like(kv), kv)
                a = a * scales.pop(u) + lax.dot_general(
                    side, weights.pop(u), (((0,), (0,)), ((), ())), preferred_element_type=F32
                )
                slots[units[u]] = (a[out : out + HDIM] * (1.0 / a[one : one + 1])).astype(BF)
        high[...] = m
        acc[...] = a

    chunk = TOKF
    parts = range(FR // 2)
    z_sent = []

    def ring_copy(ref, sems, k, d, device):
        return pltpu.make_async_remote_copy(
            src_ref=ref, dst_ref=ref, send_sem=sems[0].at[2 * (k - 1) + (d < 0)],
            recv_sem=sems[1].at[2 * (k - 1) + (d < 0)], device_id=device, device_id_type=MESH,
        )

    def z_copy(head, part, k, d, back):
        rows = pl.ds(part * chunk, chunk)
        if k == 4:
            rows = pl.ds(part * chunk + (d < 0) * (chunk // 2), chunk // 2)
        number = head * (FR // 2) + part
        ref = mzs[head].at[ring(z - d * (k - 1) - d * back, Z), rows, :]
        return ring_copy(ref, (z_send.at[number], z_recv.at[number]), k, d, zat(d))

    def w_copy(k, d, back):
        rows = pl.ds((d < 0) * HDIM, HDIM) if k == 4 else pl.ds(0, 2 * HDIM)
        ref = wbuf.at[ring(z - d * (k - 1) - d * back, Z), rows, :]
        return ring_copy(ref, (w_send, w_recv), k, d, zat(d))

    def w_start(k, d):
        w_copy(k, d, 0).start()
        z_sent.append(lambda: w_copy(k, d, 0))

    def on_w(k):
        for d in DIRS:
            w_copy(k, d, 1).wait_recv()
            if k < 4:
                w_start(k + 1, d)

    def z_start(head, part, k, d):
        z_copy(head, part, k, d, 0).start()
        z_sent.append(lambda: z_copy(head, part, k, d, 0))

    def merge(head):
        for part in parts:
            for f in (part,):
                both = jnp.concatenate([slots[last[f]], slots[last[f + FR // 2]]], axis=0)
                mzs[head][z, pl.ds(f * TOKF, TOKF), :] = both.T
            for d in DIRS:
                z_start(head, part, 1, d)
        for part in parts:
            project(head, part, z, begin=head == 0)

    def on_z(head, k):
        for part in parts:
            for d in DIRS:
                z_copy(head, part, k, d, 1).wait_recv()
                if k < 4:
                    z_start(head, part, k + 1, d)
        for part in parts:
            for d in DIRS if k < 4 else (1,):
                project(head, part, ring(z - d * k, Z))

    def project(head, part, source, begin=False):
        w = wbuf[source, pl.ds(head * HDIM, HDIM), pl.ds(pl.multiple_of(z * 128, 128), 128)]
        nil = jnp.zeros_like(w)
        wide = jnp.concatenate(
            [jnp.concatenate([w, nil], axis=1), jnp.concatenate([nil, w], axis=1)], axis=0
        )
        rows = pl.ds(part * chunk, chunk)
        term = jnp.dot(mzs[head][source, rows, :], wide, preferred_element_type=F32)
        total[rows, :] = term if begin else total[rows, :] + term

    def own(head, axis):
        (own_x if axis == "x" else own_y)(head)

    handlers.update(
        own=own, merge=merge, z=on_z, w=lambda head, k: on_w(k)
    )

    wbuf[z] = w_ref[...]
    own_x(0)
    own_y(0)
    for d in DIRS:
        w_start(1, d)
    prepare(1)
    high[...] = jnp.zeros_like(high)
    acc[...] = jnp.zeros_like(acc)
    for entry in AHEAD:
        event(*entry)
    near_done(0)

    @pl.loop(0, UNITS // PER[0])
    def _(iteration):
        for number, entry in BESIDE:
            pl.when(iteration == number)(lambda entry=entry: event(*entry))
        compute(0, iteration)

    for entry in AFTER:
        event(*entry)
    near_done(1)

    @pl.loop(0, UNITS // PER[1])
    def _(iteration):
        compute(1, iteration)

    merge(1)
    for k in (1, 2, 3, 4):
        on_z(1, k)
    for f in range(FR):
        side = f // (FR // 2)
        rows = (f % (FR // 2)) * TOKF
        o_ref[pl.ds(f * TOKF, TOKF), :] = total[
            pl.ds(rows, TOKF), pl.ds(side * 128, 128)
        ].astype(BF)
    for name in sent:
        link_copy(1, name).wait_send()
    for copy in z_sent:
        copy().wait_send()


def body(query_states, key_states, value_states, pair_list, out_weight):
    me = lax.axis_index("frames")
    both, unit, last = tables(pair_list, me)
    vmem = pl.BlockSpec(memory_space=pltpu.VMEM)
    smem = pl.BlockSpec(memory_space=pltpu.SMEM)
    return pl.pallas_call(
        kernel,
        out_shape=jax.ShapeDtypeStruct((ROWS, 128), BF),
        in_specs=[smem, smem, smem, vmem, vmem, vmem, vmem],
        out_specs=vmem,
        scratch_shapes=[
            pltpu.VMEM((DEVICES, FR, RA, 128), BF),
            pltpu.VMEM((DEVICES, FR, RA, 128), BF),
            *[pltpu.VMEM((FR, RB, 128), BF) for _ in range(16)],
            pltpu.VMEM((DEVICES + FR // 2, 2, RB, 128), BF),
            pltpu.VMEM((DEVICES + FR // 2, 2, RB, 128), BF),
            pltpu.VMEM((8, 7, 2, RB, 128), BF),
            pltpu.VMEM((8, 7, 2, RB, 128), BF),
            pltpu.VMEM((8, 2, 2, RB, 128), BF),
            pltpu.VMEM((8, 2, 2, RB, 128), BF),
            pltpu.VMEM((UNITS, HDIM, TOKF), BF),
            pltpu.VMEM((2, FR, TOKF, 128), BF),
            pltpu.VMEM((Z, FR // 2 * TOKF, 128), BF),
            pltpu.VMEM((Z, FR // 2 * TOKF, 128), BF),
            pltpu.VMEM((Z, 128, 1024), BF),
            pltpu.VMEM((FR // 2 * TOKF, 256), F32),
            pltpu.VMEM((1, TOKF), F32),
            pltpu.VMEM((128, TOKF), F32),
            pltpu.SemaphoreType.DMA((COPIES,)),
            pltpu.SemaphoreType.DMA((2,)),
            pltpu.SemaphoreType.DMA((2,)),
            pltpu.SemaphoreType.DMA((2, COPIES)),
            pltpu.SemaphoreType.DMA((8,)),
            pltpu.SemaphoreType.DMA((8,)),
            pltpu.SemaphoreType.DMA((FR, 8)),
            pltpu.SemaphoreType.DMA((FR, 8)),
        ],
        compiler_params=pltpu.CompilerParams(
            collective_id=0, has_side_effects=True, vmem_limit_bytes=63 * 2**20
        ),
        name="scene_attention",
    )(both, unit, last, query_states, key_states, value_states, out_weight)


def solution(mesh):
    placed = (
        P("frames", "heads"),
        P("frames", "heads"),
        P("frames", "heads"),
        P(),
        P("heads", None),
    )
    return jax.shard_map(
        body, mesh=mesh, in_specs=placed, out_specs=P("frames", "heads"), check_vma=False
    )
```
